32 devices in a mesh: bits: 8 (over z, core), cuts: 4 (over y, x).
Axes of the slice: x: 2, y: 2, z: 4, core: 2. Of those that a mesh axis runs over, the one named last changes fastest.
Arguments:
- boundary: float32 [4, 16384, 128], P('cuts', 'bits'), may hold values from -6 to 6
- gate_stack: float32 [34, 128, 128], replicated, may hold values from -0.5 to 0.5
- coupling: float32 [13, 128, 128], replicated, may hold values from 0.4 to 1.6
Outputs:
- probs: float32 [16384, 128], P('bits', 'cuts')
The draws below stay inside these ranges and needn't reach their ends.
All inputs are finite; a program needn't handle non-finite values.
Results may differ from the reference program's by a relative error of at most 0.00018.
Values sent between devices are 32-bit elements; how exact they have to be, the bound alone decides.
A program may use at most 64 MiB of HBM per device.

```python
import jax
import jax.numpy as jnp
from jax import lax

GATE = 128
ROWS = 2048
CYC_A = 4
CYC_B = 4
CYC_C = 5
GATES_ALL = 34
CPL_ALL = 13
ROWS_ALL = 16384
SLICES = 4
N_BITS = 8


def block_levels(own_key, dims, split, least, top_value):
    def one(position, blocks):
        steps = jax.random.uniform(jax.random.fold_in(jax.random.fold_in(own_key, 6), position), (blocks,), jnp.float32, least / len(split), top_value / len(split))
        return jnp.repeat(jnp.exp(steps), dims[position] // blocks).reshape((-1,) + (1,) * (len(dims) - position - 1))

    loudness = one(*split[0])
    for cut in split[1:]:
        loudness = loudness * one(*cut)
    return loudness


def normal_values(rng, shape, deviation, reach, cuts=(), kind=jnp.bfloat16):
    drawn = jax.random.normal(rng, shape, jnp.float32) * deviation
    if len(cuts) > 0:
        drawn = block_levels(rng, shape, cuts, -0.22, 0.18) * drawn
    return jnp.clip(drawn, min=-reach, max=reach).astype(kind)


def setup_inputs(seed: int = 0) -> dict:
    splits = jax.random.split(jax.random.key(seed), 4)
    return {
        "boundary": normal_values(splits[0], (SLICES, ROWS_ALL, GATE), 1.0, 6.0, ((0, 4), (1, 8)), jnp.float32),
        "gate_stack": normal_values(splits[1], (GATES_ALL, GATE, GATE), GATE ** -0.5, 0.5, (), jnp.float32),
        "coupling": jnp.clip(jax.random.uniform(splits[2], (CPL_ALL, GATE, GATE), jnp.float32, 0.4, 1.6), 0.4, 1.6),
    }


HIGHEST_PREC = lax.Precision.HIGHEST


def effective(weight_mat):
    order_size = weight_mat.shape[0]
    return 0.9 * jnp.eye(order_size, dtype=weight_mat.dtype) + 0.45 * weight_mat


def apply_lane(tensor, weight_mat):
    return jnp.dot(tensor, effective(weight_mat), precision=HIGHEST_PREC)


def apply_mid(tensor, weight_mat):
    order_size = weight_mat.shape[0]
    shaped = tensor.reshape(-1, order_size, tensor.shape[1])
    mixed = jnp.einsum("aic,ij->ajc", shaped, effective(weight_mat), precision=HIGHEST_PREC)
    return mixed.reshape(tensor.shape)


def apply_top(tensor, weight_mat, blocks):
    order_size = weight_mat.shape[0]
    shaped = tensor.reshape(blocks, order_size, -1)
    mixed = jnp.einsum("bir,ij->bjr", shaped, effective(weight_mat), precision=HIGHEST_PREC)
    return mixed.reshape(tensor.shape)


def apply_couple(tensor, table):
    shaped = tensor.reshape(-1, table.shape[0], tensor.shape[1])
    return (shaped * table[None]).reshape(tensor.shape)


def layer_group(tensor, gate_stack, coupling, gate_base, cpl_base, cycles, blocks):
    for turn_index in range(cycles):
        first = gate_base + 3 * turn_index
        tensor = apply_top(tensor, gate_stack[first], blocks)
        tensor = apply_lane(tensor, gate_stack[first + 1])
        tensor = apply_couple(tensor, coupling[cpl_base + turn_index])
        tensor = apply_mid(tensor, gate_stack[first + 2])
    return tensor


def final_group(tensor, gate_stack, coupling, blocks):
    gate_base = 3 * CYC_A + 3 * CYC_B
    cpl_base = CYC_A + CYC_B
    for turn_index in range(CYC_C):
        tensor = apply_top(tensor, gate_stack[gate_base + 2 * turn_index], blocks)
        tensor = apply_couple(tensor, coupling[cpl_base + turn_index])
        tensor = apply_mid(tensor, gate_stack[gate_base + 2 * turn_index + 1])
    return tensor


def swap_whole(tensor, bit_pos):
    cols = tensor.shape[1]
    shaped = tensor.reshape(N_BITS // (2 * 2 ** bit_pos), 2, 2 ** bit_pos, 2, ROWS // 2, cols)
    return jnp.swapaxes(shaped, 1, 3).reshape(tensor.shape)


def reference(boundary, gate_stack, coupling):
    top_bit = N_BITS.bit_length() - 2

    def one_slice(slice_idx, total):
        tensor = boundary[slice_idx]
        tensor = layer_group(tensor, gate_stack, coupling, 0, 0, CYC_A, N_BITS)
        tensor = swap_whole(tensor, top_bit)
        tensor = layer_group(tensor, gate_stack, coupling, 3 * CYC_A, CYC_A, CYC_B, N_BITS)
        tensor = swap_whole(tensor, 0)
        return total + tensor

    summed = lax.fori_loop(0, SLICES, one_slice, jnp.zeros(boundary.shape[1:], boundary.dtype))
    return final_group(summed, gate_stack, coupling, N_BITS)
```

```python
import functools

import jax
import jax.numpy as jnp
from jax import lax
from jax.experimental import pallas as pl
from jax.experimental.pallas import tpu as pltpu
from jax.sharding import PartitionSpec as P

MESH = pl.DeviceIdType.MESH
CYC_A = 4
CYC_B = 4
CYC_C = 5
G = 128
F32 = jnp.float32
BF16 = jnp.bfloat16


def split(x):
    hi = x.astype(BF16)
    lo = (x - hi.astype(F32)).astype(BF16)
    return hi, lo


def left_gate(w_ref, index, x):
    hi, lo = w_ref[index, 0], w_ref[index, 1]
    lhs = jnp.concatenate([jnp.concatenate([hi, hi], 1), jnp.concatenate([lo, lo], 1)], 0)
    xh, xl = split(x)
    y = jnp.dot(lhs, jnp.concatenate([xh, xl], 0), preferred_element_type=F32)
    return y[:G] + y[G:]


def right_gate(w_ref, index, x):
    row = jnp.concatenate([w_ref[index, 0], w_ref[index, 1]], 1)
    rhs = jnp.concatenate([row, row], 0)
    xh, xl = split(x)
    y = jnp.dot(jnp.concatenate([xh, xl], 1), rhs, preferred_element_type=F32)
    return y[:, :G] + y[:, G:]


def lane_blocks(shape, width):
    return lax.broadcasted_iota(jnp.int32, shape, 1) // width


def transpose_blocks(parts, width):
    n = len(parts)
    parts = list(parts)
    block = lane_blocks(parts[0].shape, width)
    m = 1
    while m < n:
        zero = (block // m) % 2 == 0
        for g in range(n):
            if g & m == 0:
                lo, hi = parts[g], parts[g | m]
                parts[g] = jnp.where(zero, lo, pltpu.roll(hi, m * width, 1))
                parts[g | m] = jnp.where(zero, pltpu.roll(lo, G - m * width, 1), hi)
        m *= 2
    return parts


def repack(src, dst, n, width):
    groups = 16 // n
    for p in range(groups):
        for q in range(groups):
            parts = transpose_blocks([src[p, q * n + h] for h in range(n)], width)
            for g in range(n):
                dst[q, p * n + g] = parts[g]


def kernel(
    n, nb, x_hbm, gate_ref, cpl_ref, out_ref,
    x, wt, wl, wm, tab, tmp, rs_buf, red, swp, sbuf, rbuf, mp, tp, in0,
    rs_send, rs_recv, swp_sem, fin_send, fin_recv, in0_sem,
):
    me = lax.axis_index("cuts")
    bit = lax.axis_index("bits")
    width = G // n
    groups = 16 // n
    top_mask = nb // 2
    par_top = (bit // top_mask) % 2
    par_low = bit % 2
    mate_top = bit + (1 - 2 * par_top) * top_mask
    mate_low = bit + 1 - 2 * par_low
    out_base = (1 - par_top) * 8
    stay_base = par_top * 8

    barrier = pltpu.get_barrier_semaphore()
    for d in range(1, n):
        pl.semaphore_signal(barrier, inc=1, device_id=(bit, lax.rem(me + d, n)), device_id_type=MESH)
    pl.semaphore_signal(barrier, inc=1, device_id=(mate_top, me), device_id_type=MESH)
    pl.semaphore_signal(barrier, inc=1, device_id=(mate_low, me), device_id_type=MESH)

    def share(ref, base, k):
        if n <= 8:
            return ref.at[pl.ds(base + k * (8 // n), 8 // n)]
        cut = n // 8
        return ref.at[base + k // cut, pl.ds((k % cut) * (16 // cut), 16 // cut)]

    eye = jnp.where(
        lax.broadcasted_iota(jnp.int32, (G, G), 0) == lax.broadcasted_iota(jnp.int32, (G, G), 1), F32(0.9), F32(0.0)
    )

    def put(w_ref, index, value):
        hi, lo = split(value)
        w_ref[index, 0] = hi
        w_ref[index, 1] = lo

    def reorder(load):
        return jnp.concatenate([load(c) for c in range(16)], 0)

    def prep_top(index, gate):
        put(wt, index, (eye + 0.45 * gate_ref[gate]).T)

    def prep_lane(index, gate):
        put(wl, index, eye + 0.45 * gate_ref[gate])

    def prep_mid(index, gate, natural=False):
        rows = reorder(lambda c: gate_ref[gate, pl.ds(c, 8, stride=16), :])
        if natural:
            diag = tmp_eye()
            put(wm, index, diag + 0.45 * rows.T)
        else:
            tmp[...] = rows.T
            put(wm, index, eye + 0.45 * reorder(lambda c: tmp[pl.ds(c, 8, stride=16), :]))

    def tmp_eye():
        r = lax.broadcasted_iota(jnp.int32, (G, G), 0)
        c = lax.broadcasted_iota(jnp.int32, (G, G), 1)
        return jnp.where((c % 8) * 16 + c // 8 == r, F32(0.9), F32(0.0))

    def prep_table(index, packed):
        value = reorder(lambda c: cpl_ref[index, pl.ds(c, 8, stride=16), :])
        if packed:
            value = jnp.where(lane_blocks((G, G), width) == me, value, 0.0)
            m = 1
            while m < n:
                value = value + pltpu.roll(value, m * width, 1)
                m *= 2
        tab[index] = value

    def prep_layers(first, count):
        @pl.loop(first, first + count)
        def _(layer):
            prep_top(layer, 3 * layer)
            prep_lane(layer, 3 * layer + 1)
            prep_mid(layer, 3 * layer + 2)

    def top(layer):
        for j in range(8):
            pair = [x[:, 2 * j + u].reshape(G, G) for u in range(2)]
            y = left_gate(wt, layer, jnp.concatenate(pair, 1))
            for u in range(2):
                x[:, 2 * j + u] = y[:, u * G:(u + 1) * G].reshape(16, 8, G)

    def lane_mid(layer, base, count):
        for j in range(0, count, 4):
            y = right_gate(wl, layer, x[pl.ds(base + j, 4)].reshape(4 * G, G))
            table = tab[layer]
            y = jnp.concatenate([y[u * G:(u + 1) * G] * table for u in range(4)], 1)
            y = left_gate(wm, layer, y)
            for u in range(4):
                x[base + j + u] = y[:, u * G:(u + 1) * G].reshape(16, 8, G)

    prep_layers(0, CYC_A)

    @pl.loop(0, CYC_A)
    def _(layer):
        prep_table(layer, False)

    for t in range(16):
        x[:, t] = x_hbm[pl.ds(t, G, stride=16), :].reshape(16, 8, G)

    @pl.loop(0, CYC_A - 1)
    def _(layer):
        top(layer)
        lane_mid(layer, 0, 16)

    top(CYC_A - 1)
    lane_mid(CYC_A - 1, out_base, 8)

    pl.semaphore_wait(barrier, n + 1)
    rs = []
    for d in range(1, n):
        to = lax.rem(me + d, n)
        rs.append(pltpu.make_async_remote_copy(
            src_ref=share(x, out_base, to), dst_ref=rs_buf.at[d - 1],
            send_sem=rs_send.at[d - 1], recv_sem=rs_recv.at[d - 1],
            device_id=(bit, to), device_id_type=MESH,
        ))
        rs[-1].start()
    lane_mid(CYC_A - 1, stay_base, 8)
    prep_layers(CYC_A, CYC_B)

    @pl.loop(CYC_A, CYC_A + CYC_B - 1)
    def _(layer):
        prep_table(layer, False)

    for copy in rs:
        copy.wait_recv()
    total = share(x, out_base, me)[...]
    for d in range(1, n):
        total = total + rs_buf[d - 1]
    red[...] = total
    swap = pltpu.make_async_remote_copy(
        src_ref=red, dst_ref=swp, send_sem=swp_sem.at[0], recv_sem=swp_sem.at[1],
        device_id=(mate_top, me), device_id_type=MESH,
    )
    swap.start()

    @pl.loop(CYC_A + CYC_B - 1, CYC_A + CYC_B + CYC_C)
    def _(layer):
        prep_table(layer, True)

    last = CYC_A + CYC_B
    @pl.loop(0, CYC_C)
    def _(turn):
        prep_top(last + turn, 3 * last + 2 * turn)

    @pl.loop(0, CYC_C - 1)
    def _(turn):
        prep_mid(last + turn, 3 * last + 2 * turn + 1)

    prep_mid(last + CYC_C - 1, 3 * last + 2 * (CYC_C - 1) + 1, natural=True)

    for copy in rs:
        copy.wait_send()
    for j in range(8):
        x[out_base + j] = jnp.zeros((16, 8, G), F32)
    swap.wait()
    share(x, out_base, me)[...] = swp[...]

    @pl.loop(CYC_A, CYC_A + CYC_B - 1)
    def _(layer):
        top(layer)
        lane_mid(layer, 0, 16)

    final = CYC_A + CYC_B - 1
    top(final)
    for p in range(groups):
        y = right_gate(wl, final, x[pl.ds(p * n, n)].reshape(n * G, G))
        parts = transpose_blocks([y[g * G:(g + 1) * G] for g in range(n)], width)
        for k in range(n):
            sbuf[k, p] = parts[k].reshape(16, 8, G)

    fin = []
    for d in range(1, n):
        to = lax.rem(me + d, n)
        fin.append(pltpu.make_async_remote_copy(
            src_ref=sbuf.at[to], dst_ref=rbuf.at[d - 1],
            send_sem=fin_send.at[d - 1], recv_sem=fin_recv.at[d - 1],
            device_id=(bit, to), device_id_type=MESH,
        ))
        fin[-1].start()
    for copy in fin:
        copy.wait_recv()

    def mid_packed(layer, load):
        table = tab[layer]
        y = jnp.concatenate([load(p) * table for p in range(groups)], 1)
        return left_gate(wm, layer, y)

    def load_sum(p):
        total = sbuf[me, p]
        for d in range(1, n):
            total = total + rbuf[d - 1, p]
        return total.reshape(G, G)

    def put_packed(ref, y):
        for p in range(groups):
            ref[p] = y[:, p * G:(p + 1) * G].reshape(16, 8, G)

    put_packed(mp, mid_packed(final, load_sum))
    repack(mp, tp, n, width)

    swap_low = pltpu.make_async_remote_copy(
        src_ref=tp.at[:, pl.ds((1 - par_low) * 8, 8)], dst_ref=in0,
        send_sem=in0_sem.at[0], recv_sem=in0_sem.at[1],
        device_id=(mate_low, me), device_id_type=MESH,
    )
    swap_low.start()
    for copy in fin:
        copy.wait_send()
    swap_low.wait()
    tp[:, pl.ds((1 - par_low) * 8, 8)] = in0[...]

    def top_packed(layer):
        y = jnp.concatenate([tp[p].reshape(G, G) for p in range(groups)], 1)
        put_packed(tp, left_gate(wt, layer, y))
        repack(tp, mp, n, width)

    @pl.loop(last, last + CYC_C - 1)
    def _(layer):
        top_packed(layer)
        put_packed(mp, mid_packed(layer, lambda p: mp[p].reshape(G, G)))
        repack(mp, tp, n, width)

    end = last + CYC_C - 1
    top_packed(end)
    y = mid_packed(end, lambda p: mp[p].reshape(G, G))
    for p in range(groups):
        part = y[:, p * G:(p + 1) * G]
        for g in range(n):
            moved = part if g == 0 else pltpu.roll(part, G - g * width, 1)
            out_ref[pl.ds((p * n + g) * G, G), :] = moved[:, :width]


def solution(mesh):
    n, nb = mesh.shape["cuts"], mesh.shape["bits"]
    groups = 16 // n
    part = (8 // n, 16, 8, G) if n <= 8 else (16 // (n // 8), 8, G)

    def on_device(boundary, gate_stack, coupling):
        vmem = pl.BlockSpec(memory_space=pltpu.VMEM)
        layers = CYC_A + CYC_B + CYC_C
        return pl.pallas_call(
            functools.partial(kernel, n, nb),
            out_shape=jax.ShapeDtypeStruct((boundary.shape[1], G // n), F32),
            in_specs=[vmem] * 3,
            out_specs=vmem,
            scratch_shapes=[
                pltpu.VMEM((16, 16, 8, G), F32),
                pltpu.VMEM((layers, 2, G, G), BF16),
                pltpu.VMEM((CYC_A + CYC_B, 2, G, G), BF16),
                pltpu.VMEM((layers, 2, G, G), BF16),
                pltpu.VMEM((layers, G, G), F32),
                pltpu.VMEM((G, G), F32),
                pltpu.VMEM((n - 1,) + part, F32),
                pltpu.VMEM(part, F32),
                pltpu.VMEM(part, F32),
                pltpu.VMEM((n, groups, 16, 8, G), F32),
                pltpu.VMEM((n - 1, groups, 16, 8, G), F32),
                pltpu.VMEM((groups, 16, 8, G), F32),
                pltpu.VMEM((groups, 16, 8, G), F32),
                pltpu.VMEM((groups, 8, 8, G), F32),
                pltpu.SemaphoreType.DMA((n - 1,)),
                pltpu.SemaphoreType.DMA((n - 1,)),
                pltpu.SemaphoreType.DMA((2,)),
                pltpu.SemaphoreType.DMA((n - 1,)),
                pltpu.SemaphoreType.DMA((n - 1,)),
                pltpu.SemaphoreType.DMA((2,)),
            ],
            compiler_params=pltpu.CompilerParams(
                collective_id=0, has_side_effects=True, vmem_limit_bytes=40 * 2**20
            ),
        )(boundary[0], gate_stack, coupling)

    return jax.shard_map(
        on_device, mesh=mesh, in_specs=(P("cuts", "bits", None), P(), P()), out_specs=P("bits", "cuts"), check_vma=False
    )
```

```python
import functools

import jax
import jax.numpy as jnp
from jax import lax
from jax.experimental import pallas as pl
from jax.experimental.pallas import tpu as pltpu
from jax.sharding import PartitionSpec as P

MESH = pl.DeviceIdType.MESH
CYC_A = 4
CYC_B = 4
CYC_C = 5
G = 128
F32 = jnp.float32
BF16 = jnp.bfloat16


def split(x):
    hi = x.astype(BF16)
    lo = (x - hi.astype(F32)).astype(BF16)
    return hi, lo


def left_gate(w_ref, index, x):
    hi, lo = w_ref[index, 0], w_ref[index, 1]
    lhs = jnp.concatenate([jnp.concatenate([hi, hi], 1), jnp.concatenate([lo, lo], 1)], 0)
    xh, xl = split(x)
    y = jnp.dot(lhs, jnp.concatenate([xh, xl], 0), preferred_element_type=F32)
    return y[:G] + y[G:]


def right_gate(w_ref, index, x):
    row = jnp.concatenate([w_ref[index, 0], w_ref[index, 1]], 1)
    rhs = jnp.concatenate([row, row], 0)
    xh, xl = split(x)
    y = jnp.dot(jnp.concatenate([xh, xl], 1), rhs, preferred_element_type=F32)
    return y[:, :G] + y[:, G:]


def lane_blocks(shape, width):
    return lax.broadcasted_iota(jnp.int32, shape, 1) // width


def transpose_blocks(parts, width):
    n = len(parts)
    parts = list(parts)
    block = lane_blocks(parts[0].shape, width)
    m = 1
    while m < n:
        zero = (block // m) % 2 == 0
        for g in range(n):
            if g & m == 0:
                lo, hi = parts[g], parts[g | m]
                parts[g] = jnp.where(zero, lo, pltpu.roll(hi, m * width, 1))
                parts[g | m] = jnp.where(zero, pltpu.roll(lo, G - m * width, 1), hi)
        m *= 2
    return parts


def repack(src, dst, n, width):
    groups = 16 // n
    for p in range(groups):
        for q in range(groups):
            parts = transpose_blocks([src[p, q * n + h] for h in range(n)], width)
            for g in range(n):
                dst[q, p * n + g] = parts[g]


def kernel(
    n, nb, x_hbm, gate_hbm, cpl_hbm, out_ref,
    x_in, gate_ref, cpl_ref, x, wt, wl, wm, tab, tmp, rs_buf, red, swp, sbuf, rbuf, mp, tp, in0,
    in_sem, rs_send, rs_recv, swp_send, swp_recv, fin_send, fin_recv, in0_sem,
):
    spans = ((0, 3), (3, 3 * CYC_A), (3 * CYC_A, gate_ref.shape[0]))
    loads = [
        pltpu.make_async_copy(gate_hbm.at[pl.ds(a, b - a)], gate_ref.at[pl.ds(a, b - a)], in_sem.at[i])
        for i, (a, b) in enumerate(spans)
    ]
    load_cpl = pltpu.make_async_copy(cpl_hbm, cpl_ref, in_sem.at[3])
    load_x = pltpu.make_async_copy(x_hbm.at[0], x_in, in_sem.at[4])
    loads[0].start()
    load_x.start()
    load_cpl.start()
    loads[1].start()
    loads[2].start()

    me = lax.axis_index("cuts")
    bit = lax.axis_index("bits")
    width = G // n
    groups = 16 // n
    top_mask = nb // 2
    par_top = (bit // top_mask) % 2
    par_low = bit % 2
    mate_top = bit + (1 - 2 * par_top) * top_mask
    mate_low = bit + 1 - 2 * par_low
    out_base = (1 - par_top) * 8
    stay_base = par_top * 8

    barrier = pltpu.get_barrier_semaphore()
    for d in range(1, n):
        pl.semaphore_signal(barrier, inc=1, device_id=(bit, lax.rem(me + d, n)), device_id_type=MESH)
    pl.semaphore_signal(barrier, inc=1, device_id=(mate_top, me), device_id_type=MESH)
    pl.semaphore_signal(barrier, inc=1, device_id=(mate_low, me), device_id_type=MESH)

    rounds = max(8 // n, 1)

    def share(ref, base, k, r):
        if n <= 8:
            return ref.at[base + k * rounds + r]
        cut = n // 8
        return ref.at[base + k // cut, pl.ds((k % cut) * (16 // cut), 16 // cut)]

    eye = jnp.where(
        lax.broadcasted_iota(jnp.int32, (G, G), 0) == lax.broadcasted_iota(jnp.int32, (G, G), 1), F32(0.9), F32(0.0)
    )

    def put(w_ref, index, value):
        hi, lo = split(value)
        w_ref[index, 0] = hi
        w_ref[index, 1] = lo

    def reorder(load):
        return jnp.concatenate([load(c) for c in range(16)], 0)

    def prep_top(index, gate):
        put(wt, index, (eye + 0.45 * gate_ref[gate]).T)

    def prep_lane(index, gate):
        put(wl, index, eye + 0.45 * gate_ref[gate])

    def prep_mid(index, gate, natural=False):
        rows = reorder(lambda c: gate_ref[gate, pl.ds(c, 8, stride=16), :])
        if natural:
            diag = tmp_eye()
            put(wm, index, diag + 0.45 * rows.T)
        else:
            tmp[...] = rows.T
            put(wm, index, eye + 0.45 * reorder(lambda c: tmp[pl.ds(c, 8, stride=16), :]))

    def tmp_eye():
        r = lax.broadcasted_iota(jnp.int32, (G, G), 0)
        c = lax.broadcasted_iota(jnp.int32, (G, G), 1)
        return jnp.where((c % 8) * 16 + c // 8 == r, F32(0.9), F32(0.0))

    def prep_table(index, packed):
        value = reorder(lambda c: cpl_ref[index, pl.ds(c, 8, stride=16), :])
        if packed:
            value = jnp.where(lane_blocks((G, G), width) == me, value, 0.0)
            m = 1
            while m < n:
                value = value + pltpu.roll(value, m * width, 1)
                m *= 2
        tab[index] = value

    def prep_layer(layer):
        prep_top(layer, 3 * layer)
        prep_lane(layer, 3 * layer + 1)
        prep_mid(layer, 3 * layer + 2)

    def prep_layers(first, count):
        pl.loop(first, first + count)(prep_layer)

    def top(layer):
        for j in range(8):
            pair = [x[:, 2 * j + u].reshape(G, G) for u in range(2)]
            y = left_gate(wt, layer, jnp.concatenate(pair, 1))
            for u in range(2):
                x[:, 2 * j + u] = y[:, u * G:(u + 1) * G].reshape(16, 8, G)

    def lane_mid(layer, blocks):
        for j in range(0, len(blocks), 4):
            y = right_gate(wl, layer, jnp.concatenate([x[blocks[j + u]].reshape(G, G) for u in range(4)], 0))
            table = tab[layer]
            y = jnp.concatenate([y[u * G:(u + 1) * G] * table for u in range(4)], 1)
            y = left_gate(wm, layer, y)
            for u in range(4):
                x[blocks[j + u]] = y[:, u * G:(u + 1) * G].reshape(16, 8, G)

    loads[0].wait()
    prep_layers(0, 1)
    load_cpl.wait()
    prep_table(0, False)
    load_x.wait()
    for t in range(16):
        x[:, t] = x_in[pl.ds(t, G, stride=16), :].reshape(16, 8, G)
    loads[1].wait()

    @pl.loop(0, CYC_A - 1)
    def _(layer):
        top(layer)
        lane_mid(layer, range(16))
        prep_layer(layer + 1)
        prep_table(layer + 1, False)

    top(CYC_A - 1)

    rs = []
    for r in range(rounds):
        if rounds == 2:
            lane_mid(CYC_A - 1, [out_base + 2 * i + r for i in range(4)])
        elif r == 0:
            lane_mid(CYC_A - 1, [out_base + i for i in range(8)])
        if r == 0:
            pl.semaphore_wait(barrier, n + 1)
        rs.append([])
        for d in range(1, n):
            to = lax.rem(me + d, n)
            rs[r].append(pltpu.make_async_remote_copy(
                src_ref=share(x, out_base, to, r), dst_ref=rs_buf.at[r, d - 1],
                send_sem=rs_send.at[r, d - 1], recv_sem=rs_recv.at[r, d - 1],
                device_id=(bit, to), device_id_type=MESH,
            ))
            rs[r][-1].start()
    lane_mid(CYC_A - 1, [stay_base + i for i in range(8)])
    loads[2].wait()

    swaps = []
    for r in range(rounds):
        for copy in rs[r]:
            copy.wait_recv()
        total = share(x, out_base, me, r)[...]
        for d in range(1, n):
            total = total + rs_buf[r, d - 1]
        red[r] = total
        swaps.append(pltpu.make_async_remote_copy(
            src_ref=red.at[r], dst_ref=swp.at[r], send_sem=swp_send.at[r], recv_sem=swp_recv.at[r],
            device_id=(mate_top, me), device_id_type=MESH,
        ))
        swaps[r].start()

    prep_layers(CYC_A, CYC_B)

    @pl.loop(CYC_A, CYC_A + CYC_B - 1)
    def _(layer):
        prep_table(layer, False)

    @pl.loop(CYC_A + CYC_B - 1, CYC_A + CYC_B + CYC_C)
    def _(layer):
        prep_table(layer, True)

    last = CYC_A + CYC_B
    @pl.loop(0, CYC_C)
    def _(turn):
        prep_top(last + turn, 3 * last + 2 * turn)

    @pl.loop(0, CYC_C - 1)
    def _(turn):
        prep_mid(last + turn, 3 * last + 2 * turn + 1)

    prep_mid(last + CYC_C - 1, 3 * last + 2 * (CYC_C - 1) + 1, natural=True)

    for r in range(rounds):
        for copy in rs[r]:
            copy.wait_send()
    for j in range(8):
        x[out_base + j] = jnp.zeros((16, 8, G), F32)
    for r in range(rounds):
        swaps[r].wait()
        share(x, out_base, me, r)[...] = swp[r]

    @pl.loop(CYC_A, CYC_A + CYC_B - 1)
    def _(layer):
        top(layer)
        lane_mid(layer, range(16))

    final = CYC_A + CYC_B - 1
    top(final)
    for p in range(groups):
        y = right_gate(wl, final, x[pl.ds(p * n, n)].reshape(n * G, G))
        parts = transpose_blocks([y[g * G:(g + 1) * G] for g in range(n)], width)
        for k in range(n):
            sbuf[k, p] = parts[k].reshape(16, 8, G)

    def send(src, dst, index, to):
        copy = pltpu.make_async_remote_copy(
            src_ref=src, dst_ref=dst, send_sem=fin_send.at[index], recv_sem=fin_recv.at[index],
            device_id=(bit, to), device_id_type=MESH,
        )
        copy.start()
        return copy

    fin = []
    if n == 4:
        near = (me + 1 - 2 * (me % 2), me + 2 - 4 * (me // 2))
        far = 3 - me
        first = [send(sbuf.at[far, p], rbuf.at[0, p], p, near[p % 2]) for p in range(groups)]
        second = [send(sbuf.at[near[p % 2], p], rbuf.at[1, p], groups + p, near[p % 2]) for p in range(groups)]
        third = []
        for p in range(groups):
            first[p].wait_recv()
            to = near[1 - p % 2]
            sbuf[to, p] = sbuf[to, p] + rbuf[0, p]
            third.append(send(sbuf.at[to, p], rbuf.at[2, p], 2 * groups + p, to))
        for copy in second + third:
            copy.wait_recv()
        fin = first + second + third
        terms = (1, 2)
    else:
        for d in range(1, n):
            to = lax.rem(me + d, n)
            fin.append(send(sbuf.at[to], rbuf.at[d - 1], d - 1, to))
        for copy in fin:
            copy.wait_recv()
        terms = range(n - 1)

    def mid_packed(layer, load):
        table = tab[layer]
        y = jnp.concatenate([load(p) * table for p in range(groups)], 1)
        return left_gate(wm, layer, y)

    def load_sum(p):
        total = sbuf[me, p]
        for d in terms:
            total = total + rbuf[d, p]
        return total.reshape(G, G)

    def put_packed(ref, y):
        for p in range(groups):
            ref[p] = y[:, p * G:(p + 1) * G].reshape(16, 8, G)

    put_packed(mp, mid_packed(final, load_sum))
    repack(mp, tp, n, width)

    swap_low = pltpu.make_async_remote_copy(
        src_ref=tp.at[:, pl.ds((1 - par_low) * 8, 8)], dst_ref=in0,
        send_sem=in0_sem.at[0], recv_sem=in0_sem.at[1],
        device_id=(mate_low, me), device_id_type=MESH,
    )
    swap_low.start()
    for copy in fin:
        copy.wait_send()
    swap_low.wait()
    tp[:, pl.ds((1 - par_low) * 8, 8)] = in0[...]

    def top_packed(layer):
        y = jnp.concatenate([tp[p].reshape(G, G) for p in range(groups)], 1)
        put_packed(tp, left_gate(wt, layer, y))
        repack(tp, mp, n, width)

    @pl.loop(last, last + CYC_C - 1)
    def _(layer):
        top_packed(layer)
        put_packed(mp, mid_packed(layer, lambda p: mp[p].reshape(G, G)))
        repack(mp, tp, n, width)

    end = last + CYC_C - 1
    top_packed(end)
    y = mid_packed(end, lambda p: mp[p].reshape(G, G))
    for p in range(groups):
        part = y[:, p * G:(p + 1) * G]
        for g in range(n):
            moved = part if g == 0 else pltpu.roll(part, G - g * width, 1)
            out_ref[pl.ds((p * n + g) * G, G), :] = moved[:, :width]


def solution(mesh):
    n, nb = mesh.shape["cuts"], mesh.shape["bits"]
    groups = 16 // n
    rounds = max(8 // n, 1)
    part = (rounds, 16 // max(n // 8, 1), 8, G)
    messages = 3 * groups if n == 4 else n - 1

    def on_device(boundary, gate_stack, coupling):
        gates, tables = gate_stack.shape[0], coupling.shape[0]
        layers = CYC_A + CYC_B + CYC_C
        return pl.pallas_call(
            functools.partial(kernel, n, nb),
            out_shape=jax.ShapeDtypeStruct((boundary.shape[1], G // n), F32),
            in_specs=[pl.BlockSpec(memory_space=pltpu.HBM)] * 3,
            out_specs=pl.BlockSpec(memory_space=pltpu.VMEM),
            scratch_shapes=[
                pltpu.VMEM(boundary.shape[1:], F32),
                pltpu.VMEM((gates, G, G), F32),
                pltpu.VMEM((tables, G, G), F32),
                pltpu.VMEM((16, 16, 8, G), F32),
                pltpu.VMEM((layers, 2, G, G), BF16),
                pltpu.VMEM((CYC_A + CYC_B, 2, G, G), BF16),
                pltpu.VMEM((layers, 2, G, G), BF16),
                pltpu.VMEM((layers, G, G), F32),
                pltpu.VMEM((G, G), F32),
                pltpu.VMEM((rounds, n - 1) + part[1:], F32),
                pltpu.VMEM(part, F32),
                pltpu.VMEM(part, F32),
                pltpu.VMEM((n, groups, 16, 8, G), F32),
                pltpu.VMEM((n - 1, groups, 16, 8, G), F32),
                pltpu.VMEM((groups, 16, 8, G), F32),
                pltpu.VMEM((groups, 16, 8, G), F32),
                pltpu.VMEM((groups, 8, 8, G), F32),
                pltpu.SemaphoreType.DMA((5,)),
                pltpu.SemaphoreType.DMA((rounds, n - 1)),
                pltpu.SemaphoreType.DMA((rounds, n - 1)),
                pltpu.SemaphoreType.DMA((rounds,)),
                pltpu.SemaphoreType.DMA((rounds,)),
                pltpu.SemaphoreType.DMA((messages,)),
                pltpu.SemaphoreType.DMA((messages,)),
                pltpu.SemaphoreType.DMA((2,)),
            ],
            compiler_params=pltpu.CompilerParams(
                collective_id=0, has_side_effects=True, vmem_limit_bytes=40 * 2**20
            ),
        )(boundary, gate_stack, coupling)

    return jax.shard_map(
        on_device, mesh=mesh, in_specs=(P("cuts", "bits", None), P(), P()), out_specs=P("bits", "cuts"), check_vma=False
    )
```

```python
import functools

import jax
import jax.numpy as jnp
from jax import lax
from jax.experimental import pallas as pl
from jax.experimental.pallas import tpu as pltpu
from jax.sharding import PartitionSpec as P

MESH = pl.DeviceIdType.MESH
CYC_A = 4
CYC_B = 4
CYC_C = 5
G = 128
F32 = jnp.float32
BF16 = jnp.bfloat16
VMEM_BYTES = 63 * 2**20 + 2**19


def split(x):
    hi = x.astype(BF16)
    lo = (x - hi.astype(F32)).astype(BF16)
    return hi, lo


def left_gate(w_ref, index, x):
    hi, lo = w_ref[index, 0], w_ref[index, 1]
    lhs = jnp.concatenate([jnp.concatenate([hi, hi], 1), jnp.concatenate([lo, lo], 1)], 0)
    xh, xl = split(x)
    y = jnp.dot(lhs, jnp.concatenate([xh, xl], 0), preferred_element_type=F32)
    return y[:G] + y[G:]


def right_gate(w_ref, index, x):
    row = jnp.concatenate([w_ref[index, 0], w_ref[index, 1]], 1)
    rhs = jnp.concatenate([row, row], 0)
    xh, xl = split(x)
    y = jnp.dot(jnp.concatenate([xh, xl], 1), rhs, preferred_element_type=F32)
    return y[:, :G] + y[:, G:]


def lane_blocks(shape, width):
    return lax.broadcasted_iota(jnp.int32, shape, 1) // width


def transpose_blocks(parts, width):
    n = len(parts)
    parts = list(parts)
    block = lane_blocks(parts[0].shape, width)
    m = 1
    while m < n:
        zero = (block // m) % 2 == 0
        for g in range(n):
            if g & m == 0:
                lo, hi = parts[g], parts[g | m]
                parts[g] = jnp.where(zero, lo, pltpu.roll(hi, m * width, 1))
                parts[g | m] = jnp.where(zero, pltpu.roll(lo, G - m * width, 1), hi)
        m *= 2
    return parts


def repack(src, dst, n, width):
    groups = 16 // n
    for p in range(groups):
        for q in range(groups):
            parts = transpose_blocks([src[p, q * n + h] for h in range(n)], width)
            for g in range(n):
                dst[q, p * n + g] = parts[g]


def kernel(
    n, nb, x_hbm, gate_hbm, cpl_hbm, out_ref,
    x_in, gate_ref, cpl_ref, x, wt, wl, wm, tab, tmp, rs_buf, red, swp, sbuf, rbuf, mp, tp, in0,
    in_sem, rs_send, rs_recv, swp_send, swp_recv, fin_send, fin_recv, in0_sem,
):
    spans = ((0, 3), (3, 3 * CYC_A), (3 * CYC_A, gate_ref.shape[0]))
    loads = [
        pltpu.make_async_copy(gate_hbm.at[pl.ds(a, b - a)], gate_ref.at[pl.ds(a, b - a)], in_sem.at[i])
        for i, (a, b) in enumerate(spans)
    ]
    load_cpl = pltpu.make_async_copy(cpl_hbm, cpl_ref, in_sem.at[3])
    load_x = pltpu.make_async_copy(x_hbm.at[0], x_in, in_sem.at[4])
    loads[0].start()
    load_x.start()
    load_cpl.start()
    loads[1].start()
    loads[2].start()

    me = lax.axis_index("cuts")
    bit = lax.axis_index("bits")
    width = G // n
    groups = 16 // n
    top_mask = nb // 2
    par_top = (bit // top_mask) % 2
    par_low = bit % 2
    mate_top = bit + (1 - 2 * par_top) * top_mask
    mate_low = bit + 1 - 2 * par_low
    out_base = (1 - par_top) * 8
    stay_base = par_top * 8

    barrier = pltpu.get_barrier_semaphore()
    for d in range(1, n):
        pl.semaphore_signal(barrier, inc=1, device_id=(bit, lax.rem(me + d, n)), device_id_type=MESH)
    pl.semaphore_signal(barrier, inc=1, device_id=(mate_top, me), device_id_type=MESH)
    pl.semaphore_signal(barrier, inc=1, device_id=(mate_low, me), device_id_type=MESH)

    rounds = max(8 // n, 1)

    def share(ref, base, k, r):
        if n <= 8:
            return ref.at[base + k * rounds + r]
        cut = n // 8
        return ref.at[base + k // cut, pl.ds((k % cut) * (16 // cut), 16 // cut)]

    eye = jnp.where(
        lax.broadcasted_iota(jnp.int32, (G, G), 0) == lax.broadcasted_iota(jnp.int32, (G, G), 1), F32(0.9), F32(0.0)
    )

    def put(w_ref, index, value):
        hi, lo = split(value)
        w_ref[index, 0] = hi
        w_ref[index, 1] = lo

    def reorder(load):
        return jnp.concatenate([load(c) for c in range(16)], 0)

    def prep_top(index, gate):
        put(wt, index, (eye + 0.45 * gate_ref[gate]).T)

    def prep_lane(index, gate):
        put(wl, index, eye + 0.45 * gate_ref[gate])

    def prep_mid(index, gate, natural=False):
        rows = reorder(lambda c: gate_ref[gate, pl.ds(c, 8, stride=16), :])
        if natural:
            diag = tmp_eye()
            put(wm, index, diag + 0.45 * rows.T)
        else:
            tmp[...] = rows.T
            put(wm, index, eye + 0.45 * reorder(lambda c: tmp[pl.ds(c, 8, stride=16), :]))

    def tmp_eye():
        r = lax.broadcasted_iota(jnp.int32, (G, G), 0)
        c = lax.broadcasted_iota(jnp.int32, (G, G), 1)
        return jnp.where((c % 8) * 16 + c // 8 == r, F32(0.9), F32(0.0))

    def prep_table(index, packed):
        value = reorder(lambda c: cpl_ref[index, pl.ds(c, 8, stride=16), :])
        if packed:
            value = jnp.where(lane_blocks((G, G), width) == me, value, 0.0)
            m = 1
            while m < n:
                value = value + pltpu.roll(value, m * width, 1)
                m *= 2
        tab[index] = value

    def prep_layer(layer):
        prep_top(layer, 3 * layer)
        prep_lane(layer, 3 * layer + 1)
        prep_mid(layer, 3 * layer + 2)

    def prep_layers(first, count):
        pl.loop(first, first + count)(prep_layer)

    def top(layer):
        for j in range(8):
            pair = [x[:, 2 * j + u].reshape(G, G) for u in range(2)]
            y = left_gate(wt, layer, jnp.concatenate(pair, 1))
            for u in range(2):
                x[:, 2 * j + u] = y[:, u * G:(u + 1) * G].reshape(16, 8, G)

    def lane_mid(layer, blocks):
        for j in range(0, len(blocks), 4):
            y = right_gate(wl, layer, jnp.concatenate([x[blocks[j + u]].reshape(G, G) for u in range(4)], 0))
            table = tab[layer]
            y = jnp.concatenate([y[u * G:(u + 1) * G] * table for u in range(4)], 1)
            y = left_gate(wm, layer, y)
            for u in range(4):
                x[blocks[j + u]] = y[:, u * G:(u + 1) * G].reshape(16, 8, G)

    loads[0].wait()
    prep_layers(0, 1)
    load_cpl.wait()
    prep_table(0, False)
    load_x.wait()
    for t in range(16):
        x[:, t] = x_in[pl.ds(t, G, stride=16), :].reshape(16, 8, G)
    loads[1].wait()

    @pl.loop(0, CYC_A - 1)
    def _(layer):
        top(layer)
        lane_mid(layer, range(16))
        prep_layer(layer + 1)
        prep_table(layer + 1, False)

    top(CYC_A - 1)

    rs = []
    for r in range(rounds):
        if rounds == 2:
            lane_mid(CYC_A - 1, [out_base + 2 * i + r for i in range(4)])
        elif r == 0:
            lane_mid(CYC_A - 1, [out_base + i for i in range(8)])
        if r == 0:
            pl.semaphore_wait(barrier, n + 1)
        rs.append([])
        for d in range(1, n):
            to = lax.rem(me + d, n)
            rs[r].append(pltpu.make_async_remote_copy(
                src_ref=share(x, out_base, to, r), dst_ref=rs_buf.at[r, d - 1],
                send_sem=rs_send.at[r, d - 1], recv_sem=rs_recv.at[r, d - 1],
                device_id=(bit, to), device_id_type=MESH,
            ))
            rs[r][-1].start()
    lane_mid(CYC_A - 1, [stay_base + i for i in range(8)])
    loads[2].wait()

    swaps = []
    for r in range(rounds):
        for copy in rs[r]:
            copy.wait_recv()
        total = share(x, out_base, me, r)[...]
        for d in range(1, n):
            total = total + rs_buf[r, d - 1]
        red[r] = total
        swaps.append(pltpu.make_async_remote_copy(
            src_ref=red.at[r], dst_ref=swp.at[r], send_sem=swp_send.at[r], recv_sem=swp_recv.at[r],
            device_id=(mate_top, me), device_id_type=MESH,
        ))
        swaps[r].start()

    prep_layers(CYC_A, CYC_B)

    @pl.loop(CYC_A, CYC_A + CYC_B - 1)
    def _(layer):
        prep_table(layer, False)

    @pl.loop(CYC_A + CYC_B - 1, CYC_A + CYC_B + CYC_C)
    def _(layer):
        prep_table(layer, True)

    last = CYC_A + CYC_B
    @pl.loop(0, CYC_C)
    def _(turn):
        prep_top(last + turn, 3 * last + 2 * turn)

    @pl.loop(0, CYC_C - 1)
    def _(turn):
        prep_mid(last + turn, 3 * last + 2 * turn + 1)

    prep_mid(last + CYC_C - 1, 3 * last + 2 * (CYC_C - 1) + 1, natural=True)

    for r in range(rounds):
        for copy in rs[r]:
            copy.wait_send()
    for j in range(8):
        x[out_base + j] = jnp.zeros((16, 8, G), F32)
    for r in range(rounds):
        swaps[r].wait()
        share(x, out_base, me, r)[...] = swp[r]

    @pl.loop(CYC_A, CYC_A + CYC_B - 1)
    def _(layer):
        top(layer)
        lane_mid(layer, range(16))

    final = CYC_A + CYC_B - 1
    top(final)
    for p in range(groups):
        y = right_gate(wl, final, x[pl.ds(p * n, n)].reshape(n * G, G))
        parts = transpose_blocks([y[g * G:(g + 1) * G] for g in range(n)], width)
        for k in range(n):
            sbuf[k, p] = parts[k].reshape(16, 8, G)

    def send(src, dst, index, to):
        copy = pltpu.make_async_remote_copy(
            src_ref=src, dst_ref=dst, send_sem=fin_send.at[index], recv_sem=fin_recv.at[index],
            device_id=(bit, to), device_id_type=MESH,
        )
        copy.start()
        return copy

    fin = []
    if n == 4:
        near = (me + 1 - 2 * (me % 2), me + 2 - 4 * (me // 2))
        far = 3 - me
        first = [send(sbuf.at[far, p], rbuf.at[0, p], p, near[p % 2]) for p in range(groups)]
        second = [send(sbuf.at[near[p % 2], p], rbuf.at[1, p], groups + p, near[p % 2]) for p in range(groups)]
        third = []
        for p in range(groups):
            first[p].wait_recv()
            to = near[1 - p % 2]
            sbuf[to, p] = sbuf[to, p] + rbuf[0, p]
            third.append(send(sbuf.at[to, p], rbuf.at[2, p], 2 * groups + p, to))
        for copy in second + third:
            copy.wait_recv()
        fin = first + second + third
        terms = (1, 2)
    else:
        for d in range(1, n):
            to = lax.rem(me + d, n)
            fin.append(send(sbuf.at[to], rbuf.at[d - 1], d - 1, to))
        for copy in fin:
            copy.wait_recv()
        terms = range(n - 1)

    def mid_packed(layer, load):
        table = tab[layer]
        y = jnp.concatenate([load(p) * table for p in range(groups)], 1)
        return left_gate(wm, layer, y)

    def load_sum(p):
        total = sbuf[me, p]
        for d in terms:
            total = total + rbuf[d, p]
        return total.reshape(G, G)

    def put_packed(ref, y):
        for p in range(groups):
            ref[p] = y[:, p * G:(p + 1) * G].reshape(16, 8, G)

    put_packed(mp, mid_packed(final, load_sum))
    repack(mp, tp, n, width)

    swap_low = pltpu.make_async_remote_copy(
        src_ref=tp.at[:, pl.ds((1 - par_low) * 8, 8)], dst_ref=in0,
        send_sem=in0_sem.at[0], recv_sem=in0_sem.at[1],
        device_id=(mate_low, me), device_id_type=MESH,
    )
    swap_low.start()
    for copy in fin:
        copy.wait_send()
    swap_low.wait()
    tp[:, pl.ds((1 - par_low) * 8, 8)] = in0[...]

    def top_packed(layer):
        y = jnp.concatenate([tp[p].reshape(G, G) for p in range(groups)], 1)
        put_packed(tp, left_gate(wt, layer, y))
        repack(tp, mp, n, width)

    @pl.loop(last, last + CYC_C - 1)
    def _(layer):
        top_packed(layer)
        put_packed(mp, mid_packed(layer, lambda p: mp[p].reshape(G, G)))
        repack(mp, tp, n, width)

    end = last + CYC_C - 1
    top_packed(end)
    y = mid_packed(end, lambda p: mp[p].reshape(G, G))
    for p in range(groups):
        part = y[:, p * G:(p + 1) * G]
        part = part.T
        for g in range(n):
            out_ref[:, (p * n + g) * G:(p * n + g + 1) * G] = part[g * width:(g + 1) * width]


def solution(mesh):
    n, nb = mesh.shape["cuts"], mesh.shape["bits"]
    groups = 16 // n
    rounds = max(8 // n, 1)
    part = (rounds, 16 // max(n // 8, 1), 8, G)
    messages = 3 * groups if n == 4 else n - 1

    def on_device(boundary, gate_stack, coupling):
        gates, tables = gate_stack.shape[0], coupling.shape[0]
        layers = CYC_A + CYC_B + CYC_C
        return pl.pallas_call(
            functools.partial(kernel, n, nb),
            out_shape=jax.ShapeDtypeStruct((G // n, boundary.shape[1]), F32),
            in_specs=[pl.BlockSpec(memory_space=pltpu.HBM)] * 3,
            out_specs=pl.BlockSpec(memory_space=pltpu.VMEM),
            scratch_shapes=[
                pltpu.VMEM(boundary.shape[1:], F32),
                pltpu.VMEM((gates, G, G), F32),
                pltpu.VMEM((tables, G, G), F32),
                pltpu.VMEM((16, 16, 8, G), F32),
                pltpu.VMEM((layers, 2, G, G), BF16),
                pltpu.VMEM((CYC_A + CYC_B, 2, G, G), BF16),
                pltpu.VMEM((layers, 2, G, G), BF16),
                pltpu.VMEM((layers, G, G), F32),
                pltpu.VMEM((G, G), F32),
                pltpu.VMEM((rounds, n - 1) + part[1:], F32),
                pltpu.VMEM(part, F32),
                pltpu.VMEM(part, F32),
                pltpu.VMEM((n, groups, 16, 8, G), F32),
                pltpu.VMEM((n - 1, groups, 16, 8, G), F32),
                pltpu.VMEM((groups, 16, 8, G), F32),
                pltpu.VMEM((groups, 16, 8, G), F32),
                pltpu.VMEM((groups, 8, 8, G), F32),
                pltpu.SemaphoreType.DMA((5,)),
                pltpu.SemaphoreType.DMA((rounds, n - 1)),
                pltpu.SemaphoreType.DMA((rounds, n - 1)),
                pltpu.SemaphoreType.DMA((rounds,)),
                pltpu.SemaphoreType.DMA((rounds,)),
                pltpu.SemaphoreType.DMA((messages,)),
                pltpu.SemaphoreType.DMA((messages,)),
                pltpu.SemaphoreType.DMA((2,)),
            ],
            compiler_params=pltpu.CompilerParams(
                collective_id=0, has_side_effects=True, vmem_limit_bytes=VMEM_BYTES
            ),
        )(boundary, gate_stack, coupling).T

    return jax.shard_map(
        on_device, mesh=mesh, in_specs=(P("cuts", "bits", None), P(), P()), out_specs=P("bits", "cuts"), check_vma=False
    )
```

```python
import functools

import jax
import jax.numpy as jnp
from jax import lax
from jax.experimental import pallas as pl
from jax.experimental.pallas import tpu as pltpu
from jax.sharding import PartitionSpec as P

MESH = pl.DeviceIdType.MESH
CYC_A = 4
CYC_B = 4
CYC_C = 5
G = 128
F32 = jnp.float32
BF16 = jnp.bfloat16
SLAB = 16
VMEM_BYTES = 63 * 2**20 + 2**18


def split(x):
    hi = x.astype(BF16)
    lo = (x - hi.astype(F32)).astype(BF16)
    return hi, lo


def left_gate(w_ref, index, x):
    w = w_ref[index]
    xh, xl = split(x)
    y = jnp.dot(jnp.concatenate([w, w], 1), jnp.concatenate([xh, xl], 0), preferred_element_type=F32)
    y = y.reshape(G // SLAB, 2, SLAB, x.shape[1])
    return (y[:, 0] + y[:, 1]).reshape(x.shape)


def right_gate(w_ref, index, x):
    row = jnp.concatenate([w_ref[index, 0], w_ref[index, 1]], 1)
    rhs = jnp.concatenate([row, row], 0)
    xh, xl = split(x)
    y = jnp.dot(jnp.concatenate([xh, xl], 1), rhs, preferred_element_type=F32)
    return y[:, :G] + y[:, G:]


def lane_blocks(shape, width):
    return lax.broadcasted_iota(jnp.int32, shape, 1) // width


def transpose_blocks(parts, width):
    n = len(parts)
    parts = list(parts)
    block = lane_blocks(parts[0].shape, width)
    m = 1
    while m < n:
        zero = (block // m) % 2 == 0
        for g in range(n):
            if g & m == 0:
                lo, hi = parts[g], parts[g | m]
                parts[g] = jnp.where(zero, lo, pltpu.roll(hi, m * width, 1))
                parts[g | m] = jnp.where(zero, pltpu.roll(lo, G - m * width, 1), hi)
        m *= 2
    return parts


def repack(src, dst, n, width):
    groups = 16 // n
    for p in range(groups):
        for q in range(groups):
            parts = transpose_blocks([src[p, q * n + h] for h in range(n)], width)
            for g in range(n):
                dst[q, p * n + g] = parts[g]


def kernel(
    n, nb, x_hbm, gate_hbm, cpl_hbm, out_ref,
    x_in, gate_ref, cpl_ref, x, wt, wl, wm, tab, tmp, rs_buf, red, swp, sbuf, rbuf, mp, tp, in0,
    in_sem, rs_send, rs_recv, swp_send, swp_recv, fin_send, fin_recv, in0_sem,
):
    spans = ((0, 3), (3, 3 * CYC_A), (3 * CYC_A, gate_ref.shape[0]))
    loads = [
        pltpu.make_async_copy(gate_hbm.at[pl.ds(a, b - a)], gate_ref.at[pl.ds(a, b - a)], in_sem.at[i])
        for i, (a, b) in enumerate(spans)
    ]
    load_cpl = pltpu.make_async_copy(cpl_hbm, cpl_ref, in_sem.at[3])
    load_x = pltpu.make_async_copy(x_hbm.at[0], x_in, in_sem.at[4])
    loads[0].start()
    load_x.start()
    load_cpl.start()
    loads[1].start()
    loads[2].start()

    me = lax.axis_index("cuts")
    bit = lax.axis_index("bits")
    width = G // n
    groups = 16 // n
    top_mask = nb // 2
    par_top = (bit // top_mask) % 2
    par_low = bit % 2
    mate_top = bit + (1 - 2 * par_top) * top_mask
    mate_low = bit + 1 - 2 * par_low
    out_base = (1 - par_top) * 8
    stay_base = par_top * 8

    barrier = pltpu.get_barrier_semaphore()
    for d in range(1, n):
        pl.semaphore_signal(barrier, inc=1, device_id=(bit, lax.rem(me + d, n)), device_id_type=MESH)
    pl.semaphore_signal(barrier, inc=1, device_id=(mate_top, me), device_id_type=MESH)
    pl.semaphore_signal(barrier, inc=1, device_id=(mate_low, me), device_id_type=MESH)

    rounds = 2 * (8 // n) if n <= 8 else 1

    def share(ref, base, k, r):
        if n <= 8:
            return ref.at[base + k * (rounds // 2) + r // 2, pl.ds(r % 2 * 8, 8)]
        cut = n // 8
        return ref.at[base + k // cut, pl.ds((k % cut) * (16 // cut), 16 // cut)]

    eye = jnp.where(
        lax.broadcasted_iota(jnp.int32, (G, G), 0) == lax.broadcasted_iota(jnp.int32, (G, G), 1), F32(0.9), F32(0.0)
    )

    def put(w_ref, index, value):
        hi, lo = split(value)
        slabs = [part[i:i + SLAB] for i in range(0, G, SLAB) for part in (hi, lo)]
        w_ref[index] = jnp.concatenate(slabs, 0)

    def reorder(load):
        return jnp.concatenate([load(c) for c in range(16)], 0)

    def prep_top(index, gate):
        put(wt, index, (eye + 0.45 * gate_ref[gate]).T)

    def prep_lane(index, gate):
        hi, lo = split(eye + 0.45 * gate_ref[gate])
        wl[index, 0] = hi
        wl[index, 1] = lo

    def prep_mid(index, gate, natural=False):
        rows = reorder(lambda c: gate_ref[gate, pl.ds(c, 8, stride=16), :])
        if natural:
            diag = tmp_eye()
            put(wm, index, diag + 0.45 * rows.T)
        else:
            tmp[...] = rows.T
            put(wm, index, eye + 0.45 * reorder(lambda c: tmp[pl.ds(c, 8, stride=16), :]))

    def tmp_eye():
        r = lax.broadcasted_iota(jnp.int32, (G, G), 0)
        c = lax.broadcasted_iota(jnp.int32, (G, G), 1)
        return jnp.where((c % 8) * 16 + c // 8 == r, F32(0.9), F32(0.0))

    def prep_table(index, packed):
        value = reorder(lambda c: cpl_ref[index, pl.ds(c, 8, stride=16), :])
        if packed:
            value = jnp.where(lane_blocks((G, G), width) == me, value, 0.0)
            m = 1
            while m < n:
                value = value + pltpu.roll(value, m * width, 1)
                m *= 2
        tab[index] = value

    def prep_layer(layer):
        prep_top(layer, 3 * layer)
        prep_lane(layer, 3 * layer + 1)
        prep_mid(layer, 3 * layer + 2)

    def prep_layers(first, count):
        pl.loop(first, first + count)(prep_layer)

    def top(layer):
        for j in range(8):
            pair = [x[:, 2 * j + u].reshape(G, G) for u in range(2)]
            y = left_gate(wt, layer, jnp.concatenate(pair, 1))
            for u in range(2):
                x[:, 2 * j + u] = y[:, u * G:(u + 1) * G].reshape(16, 8, G)

    def lane_mid(layer, blocks):
        for j in range(0, len(blocks), 4):
            y = right_gate(wl, layer, jnp.concatenate([x[blocks[j + u]].reshape(G, G) for u in range(4)], 0))
            table = tab[layer]
            for v in (0, 2):
                z = jnp.concatenate([y[u * G:(u + 1) * G] * table for u in (v, v + 1)], 1)
                z = left_gate(wm, layer, z)
                for u in range(2):
                    x[blocks[j + v + u]] = z[:, u * G:(u + 1) * G].reshape(16, 8, G)

    loads[0].wait()
    prep_layers(0, 1)
    load_cpl.wait()
    prep_table(0, False)
    load_x.wait()
    for t in range(16):
        x[:, t] = x_in[pl.ds(t, G, stride=16), :].reshape(16, 8, G)
    loads[1].wait()

    @pl.loop(0, CYC_A - 1)
    def _(layer):
        top(layer)
        lane_mid(layer, range(16))
        prep_layer(layer + 1)
        prep_table(layer + 1, False)

    top(CYC_A - 1)

    rs = []
    for r in range(rounds):
        if rounds == 4:
            if r % 2 == 0:
                lane_mid(CYC_A - 1, [out_base + 2 * i + r // 2 for i in range(4)])
        elif r == 0:
            lane_mid(CYC_A - 1, [out_base + i for i in range(8)])
        if r == 0:
            pl.semaphore_wait(barrier, n + 1)
        rs.append([])
        for d in range(1, n):
            to = lax.rem(me + d, n)
            rs[r].append(pltpu.make_async_remote_copy(
                src_ref=share(x, out_base, to, r), dst_ref=rs_buf.at[r, d - 1],
                send_sem=rs_send.at[r, d - 1], recv_sem=rs_recv.at[r, d - 1],
                device_id=(bit, to), device_id_type=MESH,
            ))
            rs[r][-1].start()
    lane_mid(CYC_A - 1, [stay_base + i for i in range(8)])
    loads[2].wait()

    swaps = []
    for r in range(rounds):
        for copy in rs[r]:
            copy.wait_recv()
        total = share(x, out_base, me, r)[...]
        for d in range(1, n):
            total = total + rs_buf[r, d - 1]
        red[r] = total
        swaps.append(pltpu.make_async_remote_copy(
            src_ref=red.at[r], dst_ref=swp.at[r], send_sem=swp_send.at[r], recv_sem=swp_recv.at[r],
            device_id=(mate_top, me), device_id_type=MESH,
        ))
        swaps[r].start()

    prep_layers(CYC_A, CYC_B)

    @pl.loop(CYC_A, CYC_A + CYC_B - 1)
    def _(layer):
        prep_table(layer, False)

    @pl.loop(CYC_A + CYC_B - 1, CYC_A + CYC_B + CYC_C)
    def _(layer):
        prep_table(layer, True)

    last = CYC_A + CYC_B
    @pl.loop(0, CYC_C)
    def _(turn):
        prep_top(last + turn, 3 * last + 2 * turn)

    @pl.loop(0, CYC_C - 1)
    def _(turn):
        prep_mid(last + turn, 3 * last + 2 * turn + 1)

    prep_mid(last + CYC_C - 1, 3 * last + 2 * (CYC_C - 1) + 1, natural=True)

    for r in range(rounds):
        for copy in rs[r]:
            copy.wait_send()
    for j in range(8):
        x[out_base + j] = jnp.zeros((16, 8, G), F32)
    for r in range(rounds):
        swaps[r].wait()
        share(x, out_base, me, r)[...] = swp[r]

    @pl.loop(CYC_A, CYC_A + CYC_B - 1)
    def _(layer):
        top(layer)
        lane_mid(layer, range(16))

    final = CYC_A + CYC_B - 1
    top(final)
    for p in range(groups):
        y = right_gate(wl, final, x[pl.ds(p * n, n)].reshape(n * G, G))
        parts = transpose_blocks([y[g * G:(g + 1) * G] for g in range(n)], width)
        for k in range(n):
            sbuf[k, p] = parts[k].reshape(16, 8, G)

    def send(src, dst, index, to):
        copy = pltpu.make_async_remote_copy(
            src_ref=src, dst_ref=dst, send_sem=fin_send.at[index], recv_sem=fin_recv.at[index],
            device_id=(bit, to), device_id_type=MESH,
        )
        copy.start()
        return copy

    fin = []
    if n == 4:
        near = (me + 1 - 2 * (me % 2), me + 2 - 4 * (me // 2))
        far = 3 - me
        first = [send(sbuf.at[far, p], rbuf.at[0, p], p, near[p % 2]) for p in range(groups)]
        second = [send(sbuf.at[near[p % 2], p], rbuf.at[1, p], groups + p, near[p % 2]) for p in range(groups)]
        third = []
        for p in range(groups):
            first[p].wait_recv()
            to = near[1 - p % 2]
            sbuf[to, p] = sbuf[to, p] + rbuf[0, p]
            third.append(send(sbuf.at[to, p], rbuf.at[2, p], 2 * groups + p, to))
        for copy in second + third:
            copy.wait_recv()
        fin = first + second + third
        terms = (1, 2)
    else:
        for d in range(1, n):
            to = lax.rem(me + d, n)
            fin.append(send(sbuf.at[to], rbuf.at[d - 1], d - 1, to))
        for copy in fin:
            copy.wait_recv()
        terms = range(n - 1)

    def mid_packed(layer, load):
        table = tab[layer]
        y = jnp.concatenate([load(p) * table for p in range(groups)], 1)
        return left_gate(wm, layer, y)

    def load_sum(p):
        total = sbuf[me, p]
        for d in terms:
            total = total + rbuf[d, p]
        return total.reshape(G, G)

    def put_packed(ref, y):
        for p in range(groups):
            ref[p] = y[:, p * G:(p + 1) * G].reshape(16, 8, G)

    put_packed(mp, mid_packed(final, load_sum))
    repack(mp, tp, n, width)

    swap_low = pltpu.make_async_remote_copy(
        src_ref=tp.at[:, pl.ds((1 - par_low) * 8, 8)], dst_ref=in0,
        send_sem=in0_sem.at[0], recv_sem=in0_sem.at[1],
        device_id=(mate_low, me), device_id_type=MESH,
    )
    swap_low.start()
    for copy in fin:
        copy.wait_send()
    swap_low.wait()
    tp[:, pl.ds((1 - par_low) * 8, 8)] = in0[...]

    def top_packed(layer):
        y = jnp.concatenate([tp[p].reshape(G, G) for p in range(groups)], 1)
        put_packed(tp, left_gate(wt, layer, y))
        repack(tp, mp, n, width)

    @pl.loop(last, last + CYC_C - 1)
    def _(layer):
        top_packed(layer)
        put_packed(mp, mid_packed(layer, lambda p: mp[p].reshape(G, G)))
        repack(mp, tp, n, width)

    end = last + CYC_C - 1
    top_packed(end)
    y = mid_packed(end, lambda p: mp[p].reshape(G, G))
    for p in range(groups):
        part = y[:, p * G:(p + 1) * G]
        part = part.T
        for g in range(n):
            out_ref[:, (p * n + g) * G:(p * n + g + 1) * G] = part[g * width:(g + 1) * width]


def solution(mesh):
    n, nb = mesh.shape["cuts"], mesh.shape["bits"]
    groups = 16 // n
    rounds = 2 * (8 // n) if n <= 8 else 1
    part = (rounds, 8 if n <= 8 else 16 // (n // 8), 8, G)
    messages = 3 * groups if n == 4 else n - 1

    def on_device(boundary, gate_stack, coupling):
        gates, tables = gate_stack.shape[0], coupling.shape[0]
        layers = CYC_A + CYC_B + CYC_C
        return pl.pallas_call(
            functools.partial(kernel, n, nb),
            out_shape=jax.ShapeDtypeStruct((G // n, boundary.shape[1]), F32),
            in_specs=[pl.BlockSpec(memory_space=pltpu.HBM)] * 3,
            out_specs=pl.BlockSpec(memory_space=pltpu.VMEM),
            scratch_shapes=[
                pltpu.VMEM(boundary.shape[1:], F32),
                pltpu.VMEM((gates, G, G), F32),
                pltpu.VMEM((tables, G, G), F32),
                pltpu.VMEM((16, 16, 8, G), F32),
                pltpu.VMEM((layers, 2 * G, G), BF16),
                pltpu.VMEM((CYC_A + CYC_B, 2, G, G), BF16),
                pltpu.VMEM((layers, 2 * G, G), BF16),
                pltpu.VMEM((layers, G, G), F32),
                pltpu.VMEM((G, G), F32),
                pltpu.VMEM((rounds, n - 1) + part[1:], F32),
                pltpu.VMEM(part, F32),
                pltpu.VMEM(part, F32),
                pltpu.VMEM((n, groups, 16, 8, G), F32),
                pltpu.VMEM((n - 1, groups, 16, 8, G), F32),
                pltpu.VMEM((groups, 16, 8, G), F32),
                pltpu.VMEM((groups, 16, 8, G), F32),
                pltpu.VMEM((groups, 8, 8, G), F32),
                pltpu.SemaphoreType.DMA((5,)),
                pltpu.SemaphoreType.DMA((rounds, n - 1)),
                pltpu.SemaphoreType.DMA((rounds, n - 1)),
                pltpu.SemaphoreType.DMA((rounds,)),
                pltpu.SemaphoreType.DMA((rounds,)),
                pltpu.SemaphoreType.DMA((messages,)),
                pltpu.SemaphoreType.DMA((messages,)),
                pltpu.SemaphoreType.DMA((2,)),
            ],
            compiler_params=pltpu.CompilerParams(
                collective_id=0, has_side_effects=True, vmem_limit_bytes=VMEM_BYTES
            ),
        )(boundary, gate_stack, coupling).T

    return jax.shard_map(
        on_device, mesh=mesh, in_specs=(P("cuts", "bits", None), P(), P()), out_specs=P("bits", "cuts"), check_vma=False
    )
```

```python
import functools

import jax
import jax.numpy as jnp
from jax import lax
from jax.experimental import pallas as pl
from jax.experimental.pallas import tpu as pltpu
from jax.sharding import PartitionSpec as P

MESH = pl.DeviceIdType.MESH
CYC_A = 4
CYC_B = 4
CYC_C = 5
G = 128
F32 = jnp.float32
BF16 = jnp.bfloat16
SLAB = 16
VMEM_BYTES = 63 * 2**20


def split(x):
    hi = x.astype(BF16)
    lo = (x - hi.astype(F32)).astype(BF16)
    return hi, lo


def left_gate(w_ref, index, x):
    w = w_ref[index]
    xh, xl = split(x)
    y = jnp.dot(jnp.concatenate([w, w], 1), jnp.concatenate([xh, xl], 0), preferred_element_type=F32)
    y = y.reshape(G // SLAB, 2, SLAB, x.shape[1])
    return (y[:, 0] + y[:, 1]).reshape(x.shape)


def right_gate(w_ref, index, x):
    row = jnp.concatenate([w_ref[index, 0], w_ref[index, 1]], 1)
    rhs = jnp.concatenate([row, row], 0)
    xh, xl = split(x)
    y = jnp.dot(jnp.concatenate([xh, xl], 1), rhs, preferred_element_type=F32)
    return y[:, :G] + y[:, G:]


def lane_blocks(shape, width):
    return lax.broadcasted_iota(jnp.int32, shape, 1) // width


def transpose_blocks(parts, width):
    n = len(parts)
    parts = list(parts)
    block = lane_blocks(parts[0].shape, width)
    m = 1
    while m < n:
        zero = (block // m) % 2 == 0
        for g in range(n):
            if g & m == 0:
                lo, hi = parts[g], parts[g | m]
                parts[g] = jnp.where(zero, lo, pltpu.roll(hi, m * width, 1))
                parts[g | m] = jnp.where(zero, pltpu.roll(lo, G - m * width, 1), hi)
        m *= 2
    return parts


def repack(src, dst, n, width):
    groups = 16 // n
    for p in range(groups):
        for q in range(groups):
            parts = transpose_blocks([src[p, q * n + h] for h in range(n)], width)
            for g in range(n):
                dst[q, p * n + g] = parts[g]


def kernel(
    n, nb, x_hbm, gate_hbm, cpl_hbm, out_ref,
    x_in, gate_ref, cpl_ref, x, wt, wl, wm, tab, tmp, rs_buf, red, swp, sbuf, rbuf, mp, tp, in0,
    in_sem, rs_send, rs_recv, swp_send, swp_recv, fin_send, fin_recv, in0_sem,
):
    spans = ((0, 3), (3, 3 * CYC_A), (3 * CYC_A, gate_ref.shape[0]))
    loads = [
        pltpu.make_async_copy(gate_hbm.at[pl.ds(a, b - a)], gate_ref.at[pl.ds(a, b - a)], in_sem.at[i])
        for i, (a, b) in enumerate(spans)
    ]
    load_cpl = pltpu.make_async_copy(cpl_hbm, cpl_ref, in_sem.at[3])
    load_x = pltpu.make_async_copy(x_hbm.at[0], x_in, in_sem.at[4])
    loads[0].start()
    load_x.start()

    me = lax.axis_index("cuts")
    bit = lax.axis_index("bits")
    width = G // n
    groups = 16 // n
    top_mask = nb // 2
    par_top = (bit // top_mask) % 2
    par_low = bit % 2
    mate_top = bit + (1 - 2 * par_top) * top_mask
    mate_low = bit + 1 - 2 * par_low
    out_base = (1 - par_top) * 8
    stay_base = par_top * 8

    barrier = pltpu.get_barrier_semaphore()
    for d in range(1, n):
        pl.semaphore_signal(barrier, inc=1, device_id=(bit, lax.rem(me + d, n)), device_id_type=MESH)
    pl.semaphore_signal(barrier, inc=1, device_id=(mate_top, me), device_id_type=MESH)
    pl.semaphore_signal(barrier, inc=1, device_id=(mate_low, me), device_id_type=MESH)

    rounds = 2 * (8 // n) if n <= 8 else 1

    def share(ref, base, k, r):
        if n <= 8:
            return ref.at[base + k * (rounds // 2) + r // 2, pl.ds(r % 2 * 8, 8)]
        cut = n // 8
        return ref.at[base + k // cut, pl.ds((k % cut) * (16 // cut), 16 // cut)]

    eye = jnp.where(
        lax.broadcasted_iota(jnp.int32, (G, G), 0) == lax.broadcasted_iota(jnp.int32, (G, G), 1), F32(0.9), F32(0.0)
    )

    def put(w_ref, index, value):
        hi, lo = split(value)
        slabs = [part[i:i + SLAB] for i in range(0, G, SLAB) for part in (hi, lo)]
        w_ref[index] = jnp.concatenate(slabs, 0)

    def reorder(load):
        return jnp.concatenate([load(c) for c in range(16)], 0)

    def prep_top(index, gate):
        put(wt, index, (eye + 0.45 * gate_ref[gate]).T)

    def prep_lane(index, gate):
        hi, lo = split(eye + 0.45 * gate_ref[gate])
        wl[index, 0] = hi
        wl[index, 1] = lo

    def prep_mid(index, gate, natural=False):
        rows = reorder(lambda c: gate_ref[gate, pl.ds(c, 8, stride=16), :])
        if natural:
            diag = tmp_eye()
            put(wm, index, diag + 0.45 * rows.T)
        else:
            tmp[...] = rows.T
            put(wm, index, eye + 0.45 * reorder(lambda c: tmp[pl.ds(c, 8, stride=16), :]))

    def tmp_eye():
        r = lax.broadcasted_iota(jnp.int32, (G, G), 0)
        c = lax.broadcasted_iota(jnp.int32, (G, G), 1)
        return jnp.where((c % 8) * 16 + c // 8 == r, F32(0.9), F32(0.0))

    def prep_table(index, packed):
        value = reorder(lambda c: cpl_ref[index, pl.ds(c, 8, stride=16), :])
        if packed:
            value = jnp.where(lane_blocks((G, G), width) == me, value, 0.0)
            m = 1
            while m < n:
                value = value + pltpu.roll(value, m * width, 1)
                m *= 2
        tab[index] = value

    def prep_layer(layer):
        prep_top(layer, 3 * layer)
        prep_lane(layer, 3 * layer + 1)
        prep_mid(layer, 3 * layer + 2)

    def prep_layers(first, count):
        pl.loop(first, first + count)(prep_layer)

    def top(layer):
        for j in range(0, 16, 4):
            y = left_gate(wt, layer, jnp.concatenate([x[:, j + u].reshape(G, G) for u in range(4)], 1))
            for u in range(4):
                x[:, j + u] = y[:, u * G:(u + 1) * G].reshape(16, 8, G)

    def lane_mid(layer, blocks):
        for j in range(0, len(blocks), 4):
            y = right_gate(wl, layer, jnp.concatenate([x[blocks[j + u]].reshape(G, G) for u in range(4)], 0))
            table = tab[layer]
            y = jnp.concatenate([y[u * G:(u + 1) * G] * table for u in range(4)], 1)
            y = left_gate(wm, layer, y)
            for u in range(4):
                x[blocks[j + u]] = y[:, u * G:(u + 1) * G].reshape(16, 8, G)

    loads[0].wait()
    prep_layers(0, 1)
    load_x.wait()
    load_cpl.start()
    loads[1].start()
    loads[2].start()
    for t in range(16):
        x[:, t] = x_in[pl.ds(t, G, stride=16), :].reshape(16, 8, G)
    load_cpl.wait()
    prep_table(0, False)
    loads[1].wait()

    @pl.loop(0, CYC_A - 1)
    def _(layer):
        top(layer)
        lane_mid(layer, range(16))
        prep_layer(layer + 1)
        prep_table(layer + 1, False)

    top(CYC_A - 1)

    rs = []
    for r in range(rounds):
        if rounds == 4:
            if r % 2 == 0:
                lane_mid(CYC_A - 1, [out_base + 2 * i + r // 2 for i in range(4)])
        elif r == 0:
            lane_mid(CYC_A - 1, [out_base + i for i in range(8)])
        if r == 0:
            pl.semaphore_wait(barrier, n + 1)
        rs.append([])
        for d in range(1, n):
            to = lax.rem(me + d, n)
            rs[r].append(pltpu.make_async_remote_copy(
                src_ref=share(x, out_base, to, r), dst_ref=rs_buf.at[r, d - 1],
                send_sem=rs_send.at[r, d - 1], recv_sem=rs_recv.at[r, d - 1],
                device_id=(bit, to), device_id_type=MESH,
            ))
            rs[r][-1].start()
    lane_mid(CYC_A - 1, [stay_base + i for i in range(8)])
    loads[2].wait()

    swaps = []
    for r in range(rounds):
        for copy in rs[r]:
            copy.wait_recv()
        total = share(x, out_base, me, r)[...]
        for d in range(1, n):
            total = total + rs_buf[r, d - 1]
        red[r] = total
        swaps.append(pltpu.make_async_remote_copy(
            src_ref=red.at[r], dst_ref=swp.at[r], send_sem=swp_send.at[r], recv_sem=swp_recv.at[r],
            device_id=(mate_top, me), device_id_type=MESH,
        ))
        swaps[r].start()

    prep_layers(CYC_A, CYC_B)

    @pl.loop(CYC_A, CYC_A + CYC_B - 1)
    def _(layer):
        prep_table(layer, False)

    @pl.loop(CYC_A + CYC_B - 1, CYC_A + CYC_B + CYC_C)
    def _(layer):
        prep_table(layer, True)

    last = CYC_A + CYC_B
    @pl.loop(0, CYC_C)
    def _(turn):
        prep_top(last + turn, 3 * last + 2 * turn)

    @pl.loop(0, CYC_C - 1)
    def _(turn):
        prep_mid(last + turn, 3 * last + 2 * turn + 1)

    prep_mid(last + CYC_C - 1, 3 * last + 2 * (CYC_C - 1) + 1, natural=True)

    for r in range(rounds):
        for copy in rs[r]:
            copy.wait_send()
    for j in range(8):
        x[out_base + j] = jnp.zeros((16, 8, G), F32)
    for r in range(rounds):
        swaps[r].wait()
        share(x, out_base, me, r)[...] = swp[r]

    @pl.loop(CYC_A, CYC_A + CYC_B - 1)
    def _(layer):
        top(layer)
        lane_mid(layer, range(16))

    final = CYC_A + CYC_B - 1
    top(final)

    def send(src, dst, index, to):
        copy = pltpu.make_async_remote_copy(
            src_ref=src, dst_ref=dst, send_sem=fin_send.at[index], recv_sem=fin_recv.at[index],
            device_id=(bit, to), device_id_type=MESH,
        )
        copy.start()
        return copy

    near = (me + 1 - 2 * (me % 2), me + 2 - 4 * (me // 2))
    far = 3 - me
    first, second, third = [], [], []
    for p in range(groups):
        y = right_gate(wl, final, x[pl.ds(p * n, n)].reshape(n * G, G))
        parts = transpose_blocks([y[g * G:(g + 1) * G] for g in range(n)], width)
        for k in range(n):
            sbuf[k, p] = parts[k].reshape(16, 8, G)
        if n == 4:
            first.append(send(sbuf.at[far, p], rbuf.at[0, p], p, near[p % 2]))
    if n == 4:
        for p in range(groups):
            second.append(send(sbuf.at[near[p % 2], p], rbuf.at[1, p], groups + p, near[p % 2]))
        for p in range(groups):
            first[p].wait_recv()
            to = near[1 - p % 2]
            sbuf[to, p] = sbuf[to, p] + rbuf[0, p]
            third.append(send(sbuf.at[to, p], rbuf.at[2, p], 2 * groups + p, to))
        terms = (1, 2)
    else:
        for d in range(1, n):
            to = lax.rem(me + d, n)
            second.append(send(sbuf.at[to], rbuf.at[d - 1], d - 1, to))
        terms = range(n - 1)
    for copy in second + third:
        copy.wait_recv()
    fin = first + second + third

    def mid_packed(layer, load):
        table = tab[layer]
        y = jnp.concatenate([load(p) * table for p in range(groups)], 1)
        return left_gate(wm, layer, y)

    def load_sum(p):
        total = sbuf[me, p]
        for d in terms:
            total = total + rbuf[d, p]
        return total.reshape(G, G)

    def put_packed(ref, y):
        for p in range(groups):
            ref[p] = y[:, p * G:(p + 1) * G].reshape(16, 8, G)

    put_packed(mp, mid_packed(final, load_sum))
    repack(mp, tp, n, width)

    swap_low = pltpu.make_async_remote_copy(
        src_ref=tp.at[:, pl.ds((1 - par_low) * 8, 8)], dst_ref=in0,
        send_sem=in0_sem.at[0], recv_sem=in0_sem.at[1],
        device_id=(mate_low, me), device_id_type=MESH,
    )
    swap_low.start()
    for copy in fin:
        copy.wait_send()
    swap_low.wait()
    tp[:, pl.ds((1 - par_low) * 8, 8)] = in0[...]

    def top_packed(layer):
        y = jnp.concatenate([tp[p].reshape(G, G) for p in range(groups)], 1)
        put_packed(tp, left_gate(wt, layer, y))
        repack(tp, mp, n, width)

    @pl.loop(last, last + CYC_C - 1)
    def _(layer):
        top_packed(layer)
        put_packed(mp, mid_packed(layer, lambda p: mp[p].reshape(G, G)))
        repack(mp, tp, n, width)

    end = last + CYC_C - 1
    top_packed(end)
    y = mid_packed(end, lambda p: mp[p].reshape(G, G))
    for p in range(groups):
        part = y[:, p * G:(p + 1) * G]
        part = part.T
        for g in range(n):
            out_ref[:, (p * n + g) * G:(p * n + g + 1) * G] = part[g * width:(g + 1) * width]


def solution(mesh):
    n, nb = mesh.shape["cuts"], mesh.shape["bits"]
    groups = 16 // n
    rounds = 2 * (8 // n) if n <= 8 else 1
    part = (rounds, 8 if n <= 8 else 16 // (n // 8), 8, G)
    messages = 3 * groups if n == 4 else n - 1

    def on_device(boundary, gate_stack, coupling):
        gates, tables = gate_stack.shape[0], coupling.shape[0]
        layers = CYC_A + CYC_B + CYC_C
        return pl.pallas_call(
            functools.partial(kernel, n, nb),
            out_shape=jax.ShapeDtypeStruct((G // n, boundary.shape[1]), F32),
            in_specs=[pl.BlockSpec(memory_space=pltpu.HBM)] * 3,
            out_specs=pl.BlockSpec(memory_space=pltpu.VMEM),
            scratch_shapes=[
                pltpu.VMEM(boundary.shape[1:], F32),
                pltpu.VMEM((gates, G, G), F32),
                pltpu.VMEM((tables, G, G), F32),
                pltpu.VMEM((16, 16, 8, G), F32),
                pltpu.VMEM((layers, 2 * G, G), BF16),
                pltpu.VMEM((CYC_A + CYC_B, 2, G, G), BF16),
                pltpu.VMEM((layers, 2 * G, G), BF16),
                pltpu.VMEM((layers, G, G), F32),
                pltpu.VMEM((G, G), F32),
                pltpu.VMEM((rounds, n - 1) + part[1:], F32),
                pltpu.VMEM(part, F32),
                pltpu.VMEM(part, F32),
                pltpu.VMEM((n, groups, 16, 8, G), F32),
                pltpu.VMEM((n - 1, groups, 16, 8, G), F32),
                pltpu.VMEM((groups, 16, 8, G), F32),
                pltpu.VMEM((groups, 16, 8, G), F32),
                pltpu.VMEM((groups, 8, 8, G), F32),
                pltpu.SemaphoreType.DMA((5,)),
                pltpu.SemaphoreType.DMA((rounds, n - 1)),
                pltpu.SemaphoreType.DMA((rounds, n - 1)),
                pltpu.SemaphoreType.DMA((rounds,)),
                pltpu.SemaphoreType.DMA((rounds,)),
                pltpu.SemaphoreType.DMA((messages,)),
                pltpu.SemaphoreType.DMA((messages,)),
                pltpu.SemaphoreType.DMA((2,)),
            ],
            compiler_params=pltpu.CompilerParams(
                collective_id=0, has_side_effects=True, vmem_limit_bytes=VMEM_BYTES
            ),
        )(boundary, gate_stack, coupling).T

    return jax.shard_map(
        on_device, mesh=mesh, in_specs=(P("cuts", "bits", None), P(), P()), out_specs=P("bits", "cuts"), check_vma=False
    )
```

```python
import functools

import jax
import jax.numpy as jnp
from jax import lax
from jax.experimental import pallas as pl
from jax.experimental.pallas import tpu as pltpu
from jax.sharding import PartitionSpec as P

MESH = pl.DeviceIdType.MESH
CYC_A = 4
CYC_B = 4
CYC_C = 5
G = 128
F32 = jnp.float32
BF16 = jnp.bfloat16
SLAB = 16
VMEM_BYTES = 63 * 2**20


def split(x):
    hi = x.astype(BF16)
    lo = (x - hi.astype(F32)).astype(BF16)
    return hi, lo


def left_gate(w_ref, index, x):
    w = w_ref[index]
    xh, xl = split(x)
    y = jnp.dot(jnp.concatenate([w, w], 1), jnp.concatenate([xh, xl], 0), preferred_element_type=F32)
    y = y.reshape(G // SLAB, 2, SLAB, x.shape[1])
    return (y[:, 0] + y[:, 1]).reshape(x.shape)


def right_gate(w_ref, index, x):
    row = jnp.concatenate([w_ref[index, 0], w_ref[index, 1]], 1)
    rhs = jnp.concatenate([row, row], 0)
    xh, xl = split(x)
    y = jnp.dot(jnp.concatenate([xh, xl], 1), rhs, preferred_element_type=F32)
    return y[:, :G] + y[:, G:]


def lane_blocks(shape, width):
    return lax.broadcasted_iota(jnp.int32, shape, 1) // width


def transpose_blocks(parts, width):
    n = len(parts)
    parts = list(parts)
    block = lane_blocks(parts[0].shape, width)
    m = 1
    while m < n:
        zero = (block // m) % 2 == 0
        for g in range(n):
            if g & m == 0:
                lo, hi = parts[g], parts[g | m]
                parts[g] = jnp.where(zero, lo, pltpu.roll(hi, m * width, 1))
                parts[g | m] = jnp.where(zero, pltpu.roll(lo, G - m * width, 1), hi)
        m *= 2
    return parts


def repack(src, dst, n, width):
    groups = 16 // n
    for p in range(groups):
        for q in range(groups):
            parts = transpose_blocks([src[p, q * n + h] for h in range(n)], width)
            for g in range(n):
                dst[q, p * n + g] = parts[g]


def kernel(
    n, nb, x_hbm, gate_hbm, cpl_hbm, out_ref,
    x_in, gate_ref, cpl_ref, x, wt, wl, wm, tab, tmp, rs_buf, red, swp, sbuf, rbuf, mp, tp, in0,
    in_sem, rs_send, rs_recv, swp_send, swp_recv, fin_send, fin_recv, in0_sem,
):
    spans = ((0, 4), (4, 3 * CYC_A + 1), (3 * CYC_A + 1, gate_ref.shape[0]))
    loads = [
        pltpu.make_async_copy(gate_hbm.at[pl.ds(a, b - a)], gate_ref.at[pl.ds(a, b - a)], in_sem.at[i])
        for i, (a, b) in enumerate(spans)
    ]
    load_cpl = pltpu.make_async_copy(cpl_hbm, cpl_ref, in_sem.at[3])
    load_x = pltpu.make_async_copy(x_hbm.at[0], x_in, in_sem.at[4])
    loads[0].start()
    load_x.start()

    me = lax.axis_index("cuts")
    bit = lax.axis_index("bits")
    width = G // n
    groups = 16 // n
    top_mask = nb // 2
    par_top = (bit // top_mask) % 2
    par_low = bit % 2
    mate_top = bit + (1 - 2 * par_top) * top_mask
    mate_low = bit + 1 - 2 * par_low
    out_base = (1 - par_top) * 8
    stay_base = par_top * 8

    barrier = pltpu.get_barrier_semaphore()
    for d in range(1, n):
        pl.semaphore_signal(barrier, inc=1, device_id=(bit, lax.rem(me + d, n)), device_id_type=MESH)
    pl.semaphore_signal(barrier, inc=1, device_id=(mate_top, me), device_id_type=MESH)
    pl.semaphore_signal(barrier, inc=1, device_id=(mate_low, me), device_id_type=MESH)

    rounds = 2 * (8 // n) if n <= 8 else 1

    def share(ref, base, k, r):
        if n <= 8:
            return ref.at[base + k * (rounds // 2) + r // 2, pl.ds(r % 2 * 8, 8)]
        cut = n // 8
        return ref.at[base + k // cut, pl.ds((k % cut) * (16 // cut), 16 // cut)]

    eye = jnp.where(
        lax.broadcasted_iota(jnp.int32, (G, G), 0) == lax.broadcasted_iota(jnp.int32, (G, G), 1), F32(0.9), F32(0.0)
    )

    def put(w_ref, index, value):
        hi, lo = split(value)
        slabs = [part[i:i + SLAB] for i in range(0, G, SLAB) for part in (hi, lo)]
        w_ref[index] = jnp.concatenate(slabs, 0)

    def reorder(load):
        return jnp.concatenate([load(c) for c in range(16)], 0)

    def prep_top(index, gate):
        put(wt, index, (eye + 0.45 * gate_ref[gate]).T)

    def prep_lane(index, gate):
        hi, lo = split(eye + 0.45 * gate_ref[gate])
        wl[index, 0] = hi
        wl[index, 1] = lo

    def prep_mid(index, gate, natural=False):
        rows = reorder(lambda c: gate_ref[gate, pl.ds(c, 8, stride=16), :])
        if natural:
            diag = tmp_eye()
            put(wm, index, diag + 0.45 * rows.T)
        else:
            tmp[...] = rows.T
            put(wm, index, eye + 0.45 * reorder(lambda c: tmp[pl.ds(c, 8, stride=16), :]))

    def tmp_eye():
        r = lax.broadcasted_iota(jnp.int32, (G, G), 0)
        c = lax.broadcasted_iota(jnp.int32, (G, G), 1)
        return jnp.where((c % 8) * 16 + c // 8 == r, F32(0.9), F32(0.0))

    def prep_table(index, packed):
        value = reorder(lambda c: cpl_ref[index, pl.ds(c, 8, stride=16), :])
        if packed:
            value = jnp.where(lane_blocks((G, G), width) == me, value, 0.0)
            m = 1
            while m < n:
                value = value + pltpu.roll(value, m * width, 1)
                m *= 2
        tab[index] = value

    def prep_layer(layer):
        prep_top(layer, 3 * layer)
        prep_lane(layer, 3 * layer + 1)
        prep_mid(layer, 3 * layer + 2)

    def prep_layers(first, count):
        pl.loop(first, first + count)(prep_layer)

    def top(layer, load=lambda t: x[:, t].reshape(G, G)):
        for j in range(0, 16, 2):
            y = left_gate(wt, layer, jnp.concatenate([load(j), load(j + 1)], 1))
            for u in range(2):
                x[:, j + u] = y[:, u * G:(u + 1) * G].reshape(16, 8, G)

    def lane_mid(layer, blocks):
        table = tab[layer]
        for j in range(0, len(blocks), 2):
            y = right_gate(wl, layer, jnp.concatenate([x[blocks[j + u]].reshape(G, G) for u in range(2)], 0))
            y = jnp.concatenate([y[u * G:(u + 1) * G] * table for u in range(2)], 1)
            y = left_gate(wm, layer, y)
            for u in range(2):
                x[blocks[j + u]] = y[:, u * G:(u + 1) * G].reshape(16, 8, G)

    loads[0].wait()
    prep_top(0, 0)
    load_x.wait()
    load_cpl.start()
    loads[1].start()
    loads[2].start()
    top(0, lambda t: x_in[pl.ds(t, G, stride=16), :])
    prep_lane(0, 1)
    prep_mid(0, 2)
    prep_top(1, 3)
    load_cpl.wait()
    prep_table(0, False)
    loads[1].wait()

    @pl.loop(0, CYC_A - 1)
    def _(layer):
        lane_mid(layer, range(16))
        top(layer + 1)
        prep_lane(layer + 1, 3 * layer + 4)
        prep_mid(layer + 1, 3 * layer + 5)
        prep_top(layer + 2, 3 * layer + 6)
        prep_table(layer + 1, False)

    rs = []
    for r in range(rounds):
        if rounds == 4:
            if r % 2 == 0:
                lane_mid(CYC_A - 1, [out_base + 2 * i + r // 2 for i in range(4)])
        elif r == 0:
            lane_mid(CYC_A - 1, [out_base + i for i in range(8)])
        if r == 0:
            pl.semaphore_wait(barrier, n + 1)
        rs.append([])
        for d in range(1, n):
            to = lax.rem(me + d, n)
            rs[r].append(pltpu.make_async_remote_copy(
                src_ref=share(x, out_base, to, r), dst_ref=rs_buf.at[r, d - 1],
                send_sem=rs_send.at[r, d - 1], recv_sem=rs_recv.at[r, d - 1],
                device_id=(bit, to), device_id_type=MESH,
            ))
            rs[r][-1].start()
    lane_mid(CYC_A - 1, [stay_base + i for i in range(8)])
    loads[2].wait()

    swaps = []
    for r in range(rounds):
        for copy in rs[r]:
            copy.wait_recv()
        total = share(x, out_base, me, r)[...]
        for d in range(1, n):
            total = total + rs_buf[r, d - 1]
        red[r] = total
        swaps.append(pltpu.make_async_remote_copy(
            src_ref=red.at[r], dst_ref=swp.at[r], send_sem=swp_send.at[r], recv_sem=swp_recv.at[r],
            device_id=(mate_top, me), device_id_type=MESH,
        ))
        swaps[r].start()

    prep_layers(CYC_A, CYC_B)

    @pl.loop(CYC_A, CYC_A + CYC_B - 1)
    def _(layer):
        prep_table(layer, False)

    @pl.loop(CYC_A + CYC_B - 1, CYC_A + CYC_B + CYC_C)
    def _(layer):
        prep_table(layer, True)

    last = CYC_A + CYC_B
    @pl.loop(0, CYC_C)
    def _(turn):
        prep_top(last + turn, 3 * last + 2 * turn)

    @pl.loop(0, CYC_C - 1)
    def _(turn):
        prep_mid(last + turn, 3 * last + 2 * turn + 1)

    prep_mid(last + CYC_C - 1, 3 * last + 2 * (CYC_C - 1) + 1, natural=True)

    for r in range(rounds):
        for copy in rs[r]:
            copy.wait_send()
    for j in range(8):
        x[out_base + j] = jnp.zeros((16, 8, G), F32)
    for r in range(rounds):
        swaps[r].wait()
        share(x, out_base, me, r)[...] = swp[r]

    top(CYC_A)

    @pl.loop(CYC_A, CYC_A + CYC_B - 1)
    def _(layer):
        lane_mid(layer, range(16))
        top(layer + 1)

    final = CYC_A + CYC_B - 1

    def send(src, dst, index, to):
        copy = pltpu.make_async_remote_copy(
            src_ref=src, dst_ref=dst, send_sem=fin_send.at[index], recv_sem=fin_recv.at[index],
            device_id=(bit, to), device_id_type=MESH,
        )
        copy.start()
        return copy

    near = (me + 1 - 2 * (me % 2), me + 2 - 4 * (me // 2))
    far = 3 - me
    first, second, third = [], [], []
    for p in range(groups):
        y = right_gate(wl, final, x[pl.ds(p * n, n)].reshape(n * G, G))
        parts = transpose_blocks([y[g * G:(g + 1) * G] for g in range(n)], width)
        for k in range(n):
            sbuf[k, p] = parts[k].reshape(16, 8, G)
        if n == 4:
            first.append(send(sbuf.at[far, p], rbuf.at[0, p], p, near[p % 2]))
    if n == 4:
        for p in range(groups):
            second.append(send(sbuf.at[near[p % 2], p], rbuf.at[1, p], groups + p, near[p % 2]))
        for p in range(groups):
            first[p].wait_recv()
            to = near[1 - p % 2]
            sbuf[to, p] = sbuf[to, p] + rbuf[0, p]
            third.append(send(sbuf.at[to, p], rbuf.at[2, p], 2 * groups + p, to))
        terms = (1, 2)
    else:
        for d in range(1, n):
            to = lax.rem(me + d, n)
            second.append(send(sbuf.at[to], rbuf.at[d - 1], d - 1, to))
        terms = range(n - 1)
    for copy in second + third:
        copy.wait_recv()
    fin = first + second + third

    def mid_packed(layer, load):
        table = tab[layer]
        y = jnp.concatenate([load(p) * table for p in range(groups)], 1)
        return left_gate(wm, layer, y)

    def load_sum(p):
        total = sbuf[me, p]
        for d in terms:
            total = total + rbuf[d, p]
        return total.reshape(G, G)

    def put_packed(ref, y):
        for p in range(groups):
            ref[p] = y[:, p * G:(p + 1) * G].reshape(16, 8, G)

    put_packed(mp, mid_packed(final, load_sum))
    repack(mp, tp, n, width)

    swap_low = pltpu.make_async_remote_copy(
        src_ref=tp.at[:, pl.ds((1 - par_low) * 8, 8)], dst_ref=in0,
        send_sem=in0_sem.at[0], recv_sem=in0_sem.at[1],
        device_id=(mate_low, me), device_id_type=MESH,
    )
    swap_low.start()
    for copy in fin:
        copy.wait_send()
    swap_low.wait()
    tp[:, pl.ds((1 - par_low) * 8, 8)] = in0[...]

    def top_packed(layer):
        y = jnp.concatenate([tp[p].reshape(G, G) for p in range(groups)], 1)
        put_packed(tp, left_gate(wt, layer, y))
        repack(tp, mp, n, width)

    @pl.loop(last, last + CYC_C - 1)
    def _(layer):
        top_packed(layer)
        put_packed(mp, mid_packed(layer, lambda p: mp[p].reshape(G, G)))
        repack(mp, tp, n, width)

    end = last + CYC_C - 1
    top_packed(end)
    y = mid_packed(end, lambda p: mp[p].reshape(G, G))
    for p in range(groups):
        part = y[:, p * G:(p + 1) * G]
        part = part.T
        for g in range(n):
            out_ref[:, (p * n + g) * G:(p * n + g + 1) * G] = part[g * width:(g + 1) * width]


def solution(mesh):
    n, nb = mesh.shape["cuts"], mesh.shape["bits"]
    groups = 16 // n
    rounds = 2 * (8 // n) if n <= 8 else 1
    part = (rounds, 8 if n <= 8 else 16 // (n // 8), 8, G)
    messages = 3 * groups if n == 4 else n - 1

    def on_device(boundary, gate_stack, coupling):
        gates, tables = gate_stack.shape[0], coupling.shape[0]
        layers = CYC_A + CYC_B + CYC_C
        return pl.pallas_call(
            functools.partial(kernel, n, nb),
            out_shape=jax.ShapeDtypeStruct((G // n, boundary.shape[1]), F32),
            in_specs=[pl.BlockSpec(memory_space=pltpu.HBM)] * 3,
            out_specs=pl.BlockSpec(memory_space=pltpu.VMEM),
            scratch_shapes=[
                pltpu.VMEM(boundary.shape[1:], F32),
                pltpu.VMEM((gates, G, G), F32),
                pltpu.VMEM((tables, G, G), F32),
                pltpu.VMEM((16, 16, 8, G), F32),
                pltpu.VMEM((layers, 2 * G, G), BF16),
                pltpu.VMEM((CYC_A + CYC_B, 2, G, G), BF16),
                pltpu.VMEM((layers, 2 * G, G), BF16),
                pltpu.VMEM((layers, G, G), F32),
                pltpu.VMEM((G, G), F32),
                pltpu.VMEM((rounds, n - 1) + part[1:], F32),
                pltpu.VMEM(part, F32),
                pltpu.VMEM(part, F32),
                pltpu.VMEM((n, groups, 16, 8, G), F32),
                pltpu.VMEM((n - 1, groups, 16, 8, G), F32),
                pltpu.VMEM((groups, 16, 8, G), F32),
                pltpu.VMEM((groups, 16, 8, G), F32),
                pltpu.VMEM((groups, 8, 8, G), F32),
                pltpu.SemaphoreType.DMA((5,)),
                pltpu.SemaphoreType.DMA((rounds, n - 1)),
                pltpu.SemaphoreType.DMA((rounds, n - 1)),
                pltpu.SemaphoreType.DMA((rounds,)),
                pltpu.SemaphoreType.DMA((rounds,)),
                pltpu.SemaphoreType.DMA((messages,)),
                pltpu.SemaphoreType.DMA((messages,)),
                pltpu.SemaphoreType.DMA((2,)),
            ],
            compiler_params=pltpu.CompilerParams(
                collective_id=0, has_side_effects=True, vmem_limit_bytes=VMEM_BYTES
            ),
        )(boundary, gate_stack, coupling).T

    return jax.shard_map(
        on_device, mesh=mesh, in_specs=(P("cuts", "bits", None), P(), P()), out_specs=P("bits", "cuts"), check_vma=False
    )
```

```python
import functools

import jax
import jax.numpy as jnp
from jax import lax
from jax.experimental import pallas as pl
from jax.experimental.pallas import tpu as pltpu
from jax.sharding import PartitionSpec as P

MESH = pl.DeviceIdType.MESH
CYC_A = 4
CYC_B = 4
CYC_C = 5
G = 128
F32 = jnp.float32
BF16 = jnp.bfloat16
VMEM_BYTES = 63 * 2**20


def split(x):
    hi = x.astype(BF16)
    lo = (x - hi.astype(F32)).astype(BF16)
    return hi, lo


def left_gate(w_ref, index, x):
    hi, lo = w_ref[index, 0], w_ref[index, 1]
    xh, xl = split(x)
    return jnp.dot(
        jnp.concatenate([hi, hi, lo], 1), jnp.concatenate([xh, xl, xh], 0), preferred_element_type=F32
    )


def right_gate(w_ref, index, x):
    row = jnp.concatenate([w_ref[index, 0], w_ref[index, 1]], 1)
    rhs = jnp.concatenate([row, row], 0)
    xh, xl = split(x)
    y = jnp.dot(jnp.concatenate([xh, xl], 1), rhs, preferred_element_type=F32)
    return y[:, :G] + y[:, G:]


def lane_blocks(shape, width):
    return lax.broadcasted_iota(jnp.int32, shape, 1) // width


def transpose_blocks(parts, width):
    n = len(parts)
    parts = list(parts)
    block = lane_blocks(parts[0].shape, width)
    m = 1
    while m < n:
        zero = (block // m) % 2 == 0
        for g in range(n):
            if g & m == 0:
                lo, hi = parts[g], parts[g | m]
                parts[g] = jnp.where(zero, lo, pltpu.roll(hi, m * width, 1))
                parts[g | m] = jnp.where(zero, pltpu.roll(lo, G - m * width, 1), hi)
        m *= 2
    return parts


def repack(src, dst, n, width):
    groups = 16 // n
    for p in range(groups):
        for q in range(groups):
            parts = transpose_blocks([src[p, q * n + h] for h in range(n)], width)
            for g in range(n):
                dst[q, p * n + g] = parts[g]


def kernel(
    n, nb, x_hbm, gate_hbm, cpl_hbm, out_ref,
    x_in, gate_ref, cpl_ref, x, wt, wl, wm, tab, tmp, rs_buf, red, swp, sbuf, rbuf, mp, tp, in0,
    in_sem, rs_send, rs_recv, swp_send, swp_recv, fin_send, fin_recv, in0_sem,
):
    spans = ((0, 4), (4, 3 * CYC_A + 1), (3 * CYC_A + 1, gate_ref.shape[0]))
    loads = [
        pltpu.make_async_copy(gate_hbm.at[pl.ds(a, b - a)], gate_ref.at[pl.ds(a, b - a)], in_sem.at[i])
        for i, (a, b) in enumerate(spans)
    ]
    load_cpl = pltpu.make_async_copy(cpl_hbm, cpl_ref, in_sem.at[3])
    load_x = pltpu.make_async_copy(x_hbm.at[0], x_in, in_sem.at[4])
    loads[0].start()
    load_x.start()
    loads[1].start()
    load_cpl.start()

    me = lax.axis_index("cuts")
    bit = lax.axis_index("bits")
    width = G // n
    groups = 16 // n
    top_mask = nb // 2
    par_top = (bit // top_mask) % 2
    par_low = bit % 2
    mate_top = bit + (1 - 2 * par_top) * top_mask
    mate_low = bit + 1 - 2 * par_low
    out_base = (1 - par_top) * 8
    stay_base = par_top * 8

    barrier = pltpu.get_barrier_semaphore()
    for d in range(1, n):
        pl.semaphore_signal(barrier, inc=1, device_id=(bit, lax.rem(me + d, n)), device_id_type=MESH)
    pl.semaphore_signal(barrier, inc=1, device_id=(mate_top, me), device_id_type=MESH)
    pl.semaphore_signal(barrier, inc=1, device_id=(mate_low, me), device_id_type=MESH)

    rounds = 2 * (8 // n) if n <= 8 else 1

    def share(ref, base, k, r):
        if n <= 8:
            return ref.at[base + k * (rounds // 2) + r // 2, pl.ds(r % 2 * 8, 8)]
        cut = n // 8
        return ref.at[base + k // cut, pl.ds((k % cut) * (16 // cut), 16 // cut)]

    eye = jnp.where(
        lax.broadcasted_iota(jnp.int32, (G, G), 0) == lax.broadcasted_iota(jnp.int32, (G, G), 1), F32(0.9), F32(0.0)
    )

    def put(w_ref, index, value):
        hi, lo = split(value)
        w_ref[index, 0] = hi
        w_ref[index, 1] = lo

    def reorder(load):
        return jnp.concatenate([load(c) for c in range(16)], 0)

    def prep_top(index, gate):
        put(wt, index, (eye + 0.45 * gate_ref[gate]).T)

    def prep_lane(index, gate):
        put(wl, index, eye + 0.45 * gate_ref[gate])

    def prep_mid(index, gate, natural=False):
        rows = reorder(lambda c: gate_ref[gate, pl.ds(c, 8, stride=16), :])
        if natural:
            diag = tmp_eye()
            put(wm, index, diag + 0.45 * rows.T)
        else:
            tmp[...] = rows.T
            put(wm, index, eye + 0.45 * reorder(lambda c: tmp[pl.ds(c, 8, stride=16), :]))

    def tmp_eye():
        r = lax.broadcasted_iota(jnp.int32, (G, G), 0)
        c = lax.broadcasted_iota(jnp.int32, (G, G), 1)
        return jnp.where((c % 8) * 16 + c // 8 == r, F32(0.9), F32(0.0))

    def prep_table(index, packed):
        value = reorder(lambda c: cpl_ref[index, pl.ds(c, 8, stride=16), :])
        if packed:
            value = jnp.where(lane_blocks((G, G), width) == me, value, 0.0)
            m = 1
            while m < n:
                value = value + pltpu.roll(value, m * width, 1)
                m *= 2
        tab[index] = value

    def prep_layer(layer):
        prep_top(layer, 3 * layer)
        prep_lane(layer, 3 * layer + 1)
        prep_mid(layer, 3 * layer + 2)

    def prep_layers(first, count):
        pl.loop(first, first + count)(prep_layer)

    def top(layer, load=lambda t: x[:, t].reshape(G, G)):
        for j in range(0, 16, 2):
            y = left_gate(wt, layer, jnp.concatenate([load(j), load(j + 1)], 1))
            for u in range(2):
                x[:, j + u] = y[:, u * G:(u + 1) * G].reshape(16, 8, G)

    def lane_mid(layer, blocks):
        table = tab[layer]
        for j in range(0, len(blocks), 2):
            y = right_gate(wl, layer, jnp.concatenate([x[blocks[j + u]].reshape(G, G) for u in range(2)], 0))
            y = jnp.concatenate([y[u * G:(u + 1) * G] * table for u in range(2)], 1)
            y = left_gate(wm, layer, y)
            for u in range(2):
                x[blocks[j + u]] = y[:, u * G:(u + 1) * G].reshape(16, 8, G)

    loads[0].wait()
    prep_top(0, 0)
    load_x.wait()
    loads[2].start()
    top(0, lambda t: x_in[pl.ds(t, G, stride=16), :])
    prep_lane(0, 1)
    prep_mid(0, 2)
    prep_top(1, 3)
    load_cpl.wait()
    prep_table(0, False)
    loads[1].wait()

    @pl.loop(0, CYC_A - 1)
    def _(layer):
        lane_mid(layer, range(16))
        top(layer + 1)
        prep_lane(layer + 1, 3 * layer + 4)
        prep_mid(layer + 1, 3 * layer + 5)
        prep_top(layer + 2, 3 * layer + 6)
        prep_table(layer + 1, False)

    rs = []
    for r in range(rounds):
        if rounds == 4:
            if r % 2 == 0:
                lane_mid(CYC_A - 1, [out_base + 2 * i + r // 2 for i in range(4)])
        elif r == 0:
            lane_mid(CYC_A - 1, [out_base + i for i in range(8)])
        if r == 0:
            pl.semaphore_wait(barrier, n + 1)
        rs.append([])
        for d in range(1, n):
            to = lax.rem(me + d, n)
            rs[r].append(pltpu.make_async_remote_copy(
                src_ref=share(x, out_base, to, r), dst_ref=rs_buf.at[r, d - 1],
                send_sem=rs_send.at[r, d - 1], recv_sem=rs_recv.at[r, d - 1],
                device_id=(bit, to), device_id_type=MESH,
            ))
            rs[r][-1].start()
    lane_mid(CYC_A - 1, [stay_base + i for i in range(8)])
    loads[2].wait()

    swaps = []
    for r in range(rounds):
        for copy in rs[r]:
            copy.wait_recv()
        total = share(x, out_base, me, r)[...]
        for d in range(1, n):
            total = total + rs_buf[r, d - 1]
        red[r] = total
        swaps.append(pltpu.make_async_remote_copy(
            src_ref=red.at[r], dst_ref=swp.at[r], send_sem=swp_send.at[r], recv_sem=swp_recv.at[r],
            device_id=(mate_top, me), device_id_type=MESH,
        ))
        swaps[r].start()

    prep_layers(CYC_A, CYC_B)

    @pl.loop(CYC_A, CYC_A + CYC_B - 1)
    def _(layer):
        prep_table(layer, False)

    @pl.loop(CYC_A + CYC_B - 1, CYC_A + CYC_B + CYC_C)
    def _(layer):
        prep_table(layer, True)

    last = CYC_A + CYC_B
    @pl.loop(0, CYC_C)
    def _(turn):
        prep_top(last + turn, 3 * last + 2 * turn)

    @pl.loop(0, CYC_C - 1)
    def _(turn):
        prep_mid(last + turn, 3 * last + 2 * turn + 1)

    prep_mid(last + CYC_C - 1, 3 * last + 2 * (CYC_C - 1) + 1, natural=True)

    for r in range(rounds):
        for copy in rs[r]:
            copy.wait_send()
    for j in range(8):
        x[out_base + j] = jnp.zeros((16, 8, G), F32)
    for r in range(rounds):
        swaps[r].wait()
        share(x, out_base, me, r)[...] = swp[r]

    top(CYC_A)

    @pl.loop(CYC_A, CYC_A + CYC_B - 1)
    def _(layer):
        lane_mid(layer, range(16))
        top(layer + 1)

    final = CYC_A + CYC_B - 1

    def send(src, dst, index, to):
        copy = pltpu.make_async_remote_copy(
            src_ref=src, dst_ref=dst, send_sem=fin_send.at[index], recv_sem=fin_recv.at[index],
            device_id=(bit, to), device_id_type=MESH,
        )
        copy.start()
        return copy

    near = (me + 1 - 2 * (me % 2), me + 2 - 4 * (me // 2))
    far = 3 - me
    first, second, third = [], [], []
    for p in range(groups):
        y = right_gate(wl, final, x[pl.ds(p * n, n)].reshape(n * G, G))
        parts = transpose_blocks([y[g * G:(g + 1) * G] for g in range(n)], width)
        for k in range(n):
            sbuf[k, p] = parts[k].reshape(16, 8, G)
        if n == 4:
            first.append(send(sbuf.at[far, p], rbuf.at[0, p], p, near[p % 2]))
    if n == 4:
        for p in range(groups):
            second.append(send(sbuf.at[near[p % 2], p], rbuf.at[1, p], groups + p, near[p % 2]))
        for p in range(groups):
            first[p].wait_recv()
            to = near[1 - p % 2]
            sbuf[to, p] = sbuf[to, p] + rbuf[0, p]
            third.append(send(sbuf.at[to, p], rbuf.at[2, p], 2 * groups + p, to))
        terms = (1, 2)
    else:
        for d in range(1, n):
            to = lax.rem(me + d, n)
            second.append(send(sbuf.at[to], rbuf.at[d - 1], d - 1, to))
        terms = range(n - 1)
    for copy in second + third:
        copy.wait_recv()
    fin = first + second + third

    def mid_packed(layer, load):
        table = tab[layer]
        y = jnp.concatenate([load(p) * table for p in range(groups)], 1)
        return left_gate(wm, layer, y)

    def load_sum(p):
        total = sbuf[me, p]
        for d in terms:
            total = total + rbuf[d, p]
        return total.reshape(G, G)

    def put_packed(ref, y):
        for p in range(groups):
            ref[p] = y[:, p * G:(p + 1) * G].reshape(16, 8, G)

    put_packed(mp, mid_packed(final, load_sum))
    repack(mp, tp, n, width)

    swap_low = pltpu.make_async_remote_copy(
        src_ref=tp.at[:, pl.ds((1 - par_low) * 8, 8)], dst_ref=in0,
        send_sem=in0_sem.at[0], recv_sem=in0_sem.at[1],
        device_id=(mate_low, me), device_id_type=MESH,
    )
    swap_low.start()
    for copy in fin:
        copy.wait_send()
    swap_low.wait()
    tp[:, pl.ds((1 - par_low) * 8, 8)] = in0[...]

    def top_packed(layer):
        y = jnp.concatenate([tp[p].reshape(G, G) for p in range(groups)], 1)
        put_packed(tp, left_gate(wt, layer, y))
        repack(tp, mp, n, width)

    @pl.loop(last, last + CYC_C - 1)
    def _(layer):
        top_packed(layer)
        put_packed(mp, mid_packed(layer, lambda p: mp[p].reshape(G, G)))
        repack(mp, tp, n, width)

    end = last + CYC_C - 1
    top_packed(end)
    y = mid_packed(end, lambda p: mp[p].reshape(G, G))
    for p in range(groups):
        part = y[:, p * G:(p + 1) * G]
        part = part.T
        for g in range(n):
            out_ref[:, (p * n + g) * G:(p * n + g + 1) * G] = part[g * width:(g + 1) * width]


def solution(mesh):
    n, nb = mesh.shape["cuts"], mesh.shape["bits"]
    groups = 16 // n
    rounds = 2 * (8 // n) if n <= 8 else 1
    part = (rounds, 8 if n <= 8 else 16 // (n // 8), 8, G)
    messages = 3 * groups if n == 4 else n - 1

    def on_device(boundary, gate_stack, coupling):
        gates, tables = gate_stack.shape[0], coupling.shape[0]
        layers = CYC_A + CYC_B + CYC_C
        return pl.pallas_call(
            functools.partial(kernel, n, nb),
            out_shape=jax.ShapeDtypeStruct((G // n, boundary.shape[1]), F32),
            in_specs=[pl.BlockSpec(memory_space=pltpu.HBM)] * 3,
            out_specs=pl.BlockSpec(memory_space=pltpu.VMEM),
            scratch_shapes=[
                pltpu.VMEM(boundary.shape[1:], F32),
                pltpu.VMEM((gates, G, G), F32),
                pltpu.VMEM((tables, G, G), F32),
                pltpu.VMEM((16, 16, 8, G), F32),
                pltpu.VMEM((layers, 2, G, G), BF16),
                pltpu.VMEM((CYC_A + CYC_B, 2, G, G), BF16),
                pltpu.VMEM((layers, 2, G, G), BF16),
                pltpu.VMEM((layers, G, G), F32),
                pltpu.VMEM((G, G), F32),
                pltpu.VMEM((rounds, n - 1) + part[1:], F32),
                pltpu.VMEM(part, F32),
                pltpu.VMEM(part, F32),
                pltpu.VMEM((n, groups, 16, 8, G), F32),
                pltpu.VMEM((n - 1, groups, 16, 8, G), F32),
                pltpu.VMEM((groups, 16, 8, G), F32),
                pltpu.VMEM((groups, 16, 8, G), F32),
                pltpu.VMEM((groups, 8, 8, G), F32),
                pltpu.SemaphoreType.DMA((5,)),
                pltpu.SemaphoreType.DMA((rounds, n - 1)),
                pltpu.SemaphoreType.DMA((rounds, n - 1)),
                pltpu.SemaphoreType.DMA((rounds,)),
                pltpu.SemaphoreType.DMA((rounds,)),
                pltpu.SemaphoreType.DMA((messages,)),
                pltpu.SemaphoreType.DMA((messages,)),
                pltpu.SemaphoreType.DMA((2,)),
            ],
            compiler_params=pltpu.CompilerParams(
                collective_id=0, has_side_effects=True, vmem_limit_bytes=VMEM_BYTES
            ),
        )(boundary, gate_stack, coupling).T

    return jax.shard_map(
        on_device, mesh=mesh, in_specs=(P("cuts", "bits", None), P(), P()), out_specs=P("bits", "cuts"), check_vma=False
    )
```

```python
import functools

import jax
import jax.numpy as jnp
from jax import lax
from jax.experimental import pallas as pl
from jax.experimental.pallas import tpu as pltpu
from jax.sharding import PartitionSpec as P

MESH = pl.DeviceIdType.MESH
CYC_A = 4
CYC_B = 4
CYC_C = 5
G = 128
F32 = jnp.float32
BF16 = jnp.bfloat16
VMEM_BYTES = 63 * 2**20


def split(x):
    hi = x.astype(BF16)
    lo = (x - hi.astype(F32)).astype(BF16)
    return hi, lo


def left_gate(w_ref, index, x):
    hi, lo = w_ref[index, 0], w_ref[index, 1]
    xh, xl = split(x)
    return jnp.dot(
        jnp.concatenate([hi, hi, lo], 1), jnp.concatenate([xh, xl, xh], 0), preferred_element_type=F32
    )


def right_gate(w_ref, index, x):
    row = jnp.concatenate([w_ref[index, 0], w_ref[index, 1]], 1)
    rhs = jnp.concatenate([row, row], 0)
    xh, xl = split(x)
    y = jnp.dot(jnp.concatenate([xh, xl], 1), rhs, preferred_element_type=F32)
    return y[:, :G] + y[:, G:]


def lane_blocks(shape, width):
    return lax.broadcasted_iota(jnp.int32, shape, 1) // width


def transpose_blocks(parts, width):
    n = len(parts)
    parts = list(parts)
    block = lane_blocks(parts[0].shape, width)
    m = 1
    while m < n:
        zero = (block // m) % 2 == 0
        for g in range(n):
            if g & m == 0:
                lo, hi = parts[g], parts[g | m]
                parts[g] = jnp.where(zero, lo, pltpu.roll(hi, m * width, 1))
                parts[g | m] = jnp.where(zero, pltpu.roll(lo, G - m * width, 1), hi)
        m *= 2
    return parts


def repack(src, dst, n, width):
    groups = 16 // n
    for p in range(groups):
        for q in range(groups):
            parts = transpose_blocks([src[p, q * n + h] for h in range(n)], width)
            for g in range(n):
                dst[q, p * n + g] = parts[g]


def kernel(
    n, nb, x_hbm, gate_hbm, cpl_hbm, out_ref,
    x_in, gate_ref, cpl_ref, x, wt, wl, wm, tab, tmp, rs_buf, red, swp, sbuf, rbuf, mp, tp, in0,
    in_sem, rs_send, rs_recv, swp_send, swp_recv, fin_send, fin_recv, in0_sem,
):
    spans = ((0, 4), (4, 3 * CYC_A + 1), (3 * CYC_A + 1, gate_ref.shape[0]))
    loads = [
        pltpu.make_async_copy(gate_hbm.at[pl.ds(a, b - a)], gate_ref.at[pl.ds(a, b - a)], in_sem.at[i])
        for i, (a, b) in enumerate(spans)
    ]
    load_cpl = pltpu.make_async_copy(cpl_hbm, cpl_ref, in_sem.at[3])
    load_x = pltpu.make_async_copy(x_hbm.at[0], x_in, in_sem.at[4])
    loads[0].start()
    load_x.start()
    loads[1].start()
    load_cpl.start()

    me = lax.axis_index("cuts")
    bit = lax.axis_index("bits")
    width = G // n
    groups = 16 // n
    top_mask = nb // 2
    par_top = (bit // top_mask) % 2
    par_low = bit % 2
    mate_top = bit + (1 - 2 * par_top) * top_mask
    mate_low = bit + 1 - 2 * par_low
    out_base = (1 - par_top) * 8
    stay_base = par_top * 8

    barrier = pltpu.get_barrier_semaphore()
    for d in range(1, n):
        pl.semaphore_signal(barrier, inc=1, device_id=(bit, lax.rem(me + d, n)), device_id_type=MESH)
    pl.semaphore_signal(barrier, inc=1, device_id=(mate_top, me), device_id_type=MESH)
    pl.semaphore_signal(barrier, inc=1, device_id=(mate_low, me), device_id_type=MESH)

    rounds = 2 * (8 // n) if n <= 8 else 1

    def share(ref, base, k, r):
        if n <= 8:
            return ref.at[base + k * (rounds // 2) + r // 2, pl.ds(r % 2 * 8, 8)]
        cut = n // 8
        return ref.at[base + k // cut, pl.ds((k % cut) * (16 // cut), 16 // cut)]

    eye = jnp.where(
        lax.broadcasted_iota(jnp.int32, (G, G), 0) == lax.broadcasted_iota(jnp.int32, (G, G), 1), F32(0.9), F32(0.0)
    )

    def put(w_ref, index, value):
        hi, lo = split(value)
        w_ref[index, 0] = hi
        w_ref[index, 1] = lo

    def reorder(load):
        return jnp.concatenate([load(c) for c in range(16)], 0)

    def prep_top(index, gate):
        put(wt, index, (eye + 0.45 * gate_ref[gate]).T)

    def prep_lane(index, gate):
        put(wl, index, eye + 0.45 * gate_ref[gate])

    def prep_mid(index, gate, natural=False):
        rows = reorder(lambda c: gate_ref[gate, pl.ds(c, 8, stride=16), :])
        if natural:
            diag = tmp_eye()
            put(wm, index, diag + 0.45 * rows.T)
        else:
            tmp[...] = rows.T
            put(wm, index, eye + 0.45 * reorder(lambda c: tmp[pl.ds(c, 8, stride=16), :]))

    def tmp_eye():
        r = lax.broadcasted_iota(jnp.int32, (G, G), 0)
        c = lax.broadcasted_iota(jnp.int32, (G, G), 1)
        return jnp.where((c % 8) * 16 + c // 8 == r, F32(0.9), F32(0.0))

    def prep_table(index, packed):
        value = reorder(lambda c: cpl_ref[index, pl.ds(c, 8, stride=16), :])
        if packed:
            value = jnp.where(lane_blocks((G, G), width) == me, value, 0.0)
            m = 1
            while m < n:
                value = value + pltpu.roll(value, m * width, 1)
                m *= 2
        tab[index] = value

    def prep_layer(layer):
        prep_top(layer, 3 * layer)
        prep_lane(layer, 3 * layer + 1)
        prep_mid(layer, 3 * layer + 2)

    def prep_layers(first, count):
        pl.loop(first, first + count)(prep_layer)

    def top(layer, load=lambda t: x[:, t].reshape(G, G)):
        @pl.loop(0, 4)
        def _(step):
            for j in (4 * step, 4 * step + 2):
                y = left_gate(wt, layer, jnp.concatenate([load(j), load(j + 1)], 1))
                for u in range(2):
                    x[:, j + u] = y[:, u * G:(u + 1) * G].reshape(16, 8, G)

    def lane_mid(layer, blocks):
        table = tab[layer]
        for j in range(0, len(blocks), 2):
            y = right_gate(wl, layer, jnp.concatenate([x[blocks[j + u]].reshape(G, G) for u in range(2)], 0))
            y = jnp.concatenate([y[u * G:(u + 1) * G] * table for u in range(2)], 1)
            y = left_gate(wm, layer, y)
            for u in range(2):
                x[blocks[j + u]] = y[:, u * G:(u + 1) * G].reshape(16, 8, G)

    loads[0].wait()
    prep_top(0, 0)
    load_x.wait()
    loads[2].start()
    top(0, lambda t: x_in[pl.ds(t, G, stride=16), :])
    prep_lane(0, 1)
    prep_mid(0, 2)
    prep_top(1, 3)
    load_cpl.wait()
    prep_table(0, False)
    loads[1].wait()

    def lane_mid_run(layer, base, count):
        @pl.loop(0, count // 4)
        def _(step):
            lane_mid(layer, [base + 4 * step + u for u in range(4)])

    @pl.loop(0, CYC_A - 1)
    def _(layer):
        lane_mid_run(layer, 0, 16)
        top(layer + 1)
        prep_lane(layer + 1, 3 * layer + 4)
        prep_mid(layer + 1, 3 * layer + 5)
        prep_top(layer + 2, 3 * layer + 6)
        prep_table(layer + 1, False)

    rs = []
    for r in range(rounds):
        if rounds == 4:
            if r % 2 == 0:
                lane_mid(CYC_A - 1, [out_base + 2 * i + r // 2 for i in range(4)])
        elif r == 0:
            lane_mid(CYC_A - 1, [out_base + i for i in range(8)])
        if r == 0:
            pl.semaphore_wait(barrier, n + 1)
        rs.append([])
        for d in range(1, n):
            to = lax.rem(me + d, n)
            rs[r].append(pltpu.make_async_remote_copy(
                src_ref=share(x, out_base, to, r), dst_ref=rs_buf.at[r, d - 1],
                send_sem=rs_send.at[r, d - 1], recv_sem=rs_recv.at[r, d - 1],
                device_id=(bit, to), device_id_type=MESH,
            ))
            rs[r][-1].start()
    lane_mid_run(CYC_A - 1, stay_base, 8)
    loads[2].wait()

    swaps = []
    for r in range(rounds):
        for copy in rs[r]:
            copy.wait_recv()
        total = share(x, out_base, me, r)[...]
        for d in range(1, n):
            total = total + rs_buf[r, d - 1]
        red[r] = total
        swaps.append(pltpu.make_async_remote_copy(
            src_ref=red.at[r], dst_ref=swp.at[r], send_sem=swp_send.at[r], recv_sem=swp_recv.at[r],
            device_id=(mate_top, me), device_id_type=MESH,
        ))
        swaps[r].start()

    prep_layers(CYC_A, CYC_B)

    @pl.loop(CYC_A, CYC_A + CYC_B - 1)
    def _(layer):
        prep_table(layer, False)

    @pl.loop(CYC_A + CYC_B - 1, CYC_A + CYC_B + CYC_C)
    def _(layer):
        prep_table(layer, True)

    last = CYC_A + CYC_B
    @pl.loop(0, CYC_C)
    def _(turn):
        prep_top(last + turn, 3 * last + 2 * turn)

    @pl.loop(0, CYC_C - 1)
    def _(turn):
        prep_mid(last + turn, 3 * last + 2 * turn + 1)

    prep_mid(last + CYC_C - 1, 3 * last + 2 * (CYC_C - 1) + 1, natural=True)

    for r in range(rounds):
        for copy in rs[r]:
            copy.wait_send()
    for j in range(8):
        x[out_base + j] = jnp.zeros((16, 8, G), F32)
    for r in range(rounds):
        swaps[r].wait()
        share(x, out_base, me, r)[...] = swp[r]

    top(CYC_A)

    @pl.loop(CYC_A, CYC_A + CYC_B - 1)
    def _(layer):
        lane_mid_run(layer, 0, 16)
        top(layer + 1)

    final = CYC_A + CYC_B - 1

    def send(src, dst, index, to):
        copy = pltpu.make_async_remote_copy(
            src_ref=src, dst_ref=dst, send_sem=fin_send.at[index], recv_sem=fin_recv.at[index],
            device_id=(bit, to), device_id_type=MESH,
        )
        copy.start()
        return copy

    near = (me + 1 - 2 * (me % 2), me + 2 - 4 * (me // 2))
    far = 3 - me
    first, second, third = [], [], []
    for p in range(groups):
        y = right_gate(wl, final, x[pl.ds(p * n, n)].reshape(n * G, G))
        parts = transpose_blocks([y[g * G:(g + 1) * G] for g in range(n)], width)
        for k in range(n):
            sbuf[k, p] = parts[k].reshape(16, 8, G)
        if n == 4:
            first.append(send(sbuf.at[far, p], rbuf.at[0, p], p, near[p % 2]))
    if n == 4:
        for p in range(groups):
            second.append(send(sbuf.at[near[p % 2], p], rbuf.at[1, p], groups + p, near[p % 2]))
        for p in range(groups):
            first[p].wait_recv()
            to = near[1 - p % 2]
            sbuf[to, p] = sbuf[to, p] + rbuf[0, p]
            third.append(send(sbuf.at[to, p], rbuf.at[2, p], 2 * groups + p, to))
        terms = (1, 2)
    else:
        for d in range(1, n):
            to = lax.rem(me + d, n)
            second.append(send(sbuf.at[to], rbuf.at[d - 1], d - 1, to))
        terms = range(n - 1)
    for copy in second + third:
        copy.wait_recv()
    fin = first + second + third

    def mid_packed(layer, load):
        table = tab[layer]
        y = jnp.concatenate([load(p) * table for p in range(groups)], 1)
        return left_gate(wm, layer, y)

    def load_sum(p):
        total = sbuf[me, p]
        for d in terms:
            total = total + rbuf[d, p]
        return total.reshape(G, G)

    def put_packed(ref, y):
        for p in range(groups):
            ref[p] = y[:, p * G:(p + 1) * G].reshape(16, 8, G)

    put_packed(mp, mid_packed(final, load_sum))
    repack(mp, tp, n, width)

    swap_low = pltpu.make_async_remote_copy(
        src_ref=tp.at[:, pl.ds((1 - par_low) * 8, 8)], dst_ref=in0,
        send_sem=in0_sem.at[0], recv_sem=in0_sem.at[1],
        device_id=(mate_low, me), device_id_type=MESH,
    )
    swap_low.start()
    for copy in fin:
        copy.wait_send()
    swap_low.wait()
    tp[:, pl.ds((1 - par_low) * 8, 8)] = in0[...]

    def top_packed(layer):
        y = jnp.concatenate([tp[p].reshape(G, G) for p in range(groups)], 1)
        put_packed(tp, left_gate(wt, layer, y))
        repack(tp, mp, n, width)

    @pl.loop(last, last + CYC_C - 1)
    def _(layer):
        top_packed(layer)
        put_packed(mp, mid_packed(layer, lambda p: mp[p].reshape(G, G)))
        repack(mp, tp, n, width)

    end = last + CYC_C - 1
    top_packed(end)
    y = mid_packed(end, lambda p: mp[p].reshape(G, G))
    for p in range(groups):
        part = y[:, p * G:(p + 1) * G]
        part = part.T
        for g in range(n):
            out_ref[:, (p * n + g) * G:(p * n + g + 1) * G] = part[g * width:(g + 1) * width]


def solution(mesh):
    n, nb = mesh.shape["cuts"], mesh.shape["bits"]
    groups = 16 // n
    rounds = 2 * (8 // n) if n <= 8 else 1
    part = (rounds, 8 if n <= 8 else 16 // (n // 8), 8, G)
    messages = 3 * groups if n == 4 else n - 1

    def on_device(boundary, gate_stack, coupling):
        gates, tables = gate_stack.shape[0], coupling.shape[0]
        layers = CYC_A + CYC_B + CYC_C
        return pl.pallas_call(
            functools.partial(kernel, n, nb),
            out_shape=jax.ShapeDtypeStruct((G // n, boundary.shape[1]), F32),
            in_specs=[pl.BlockSpec(memory_space=pltpu.HBM)] * 3,
            out_specs=pl.BlockSpec(memory_space=pltpu.VMEM),
            scratch_shapes=[
                pltpu.VMEM(boundary.shape[1:], F32),
                pltpu.VMEM((gates, G, G), F32),
                pltpu.VMEM((tables, G, G), F32),
                pltpu.VMEM((16, 16, 8, G), F32),
                pltpu.VMEM((layers, 2, G, G), BF16),
                pltpu.VMEM((CYC_A + CYC_B, 2, G, G), BF16),
                pltpu.VMEM((layers, 2, G, G), BF16),
                pltpu.VMEM((layers, G, G), F32),
                pltpu.VMEM((G, G), F32),
                pltpu.VMEM((rounds, n - 1) + part[1:], F32),
                pltpu.VMEM(part, F32),
                pltpu.VMEM(part, F32),
                pltpu.VMEM((n, groups, 16, 8, G), F32),
                pltpu.VMEM((n - 1, groups, 16, 8, G), F32),
                pltpu.VMEM((groups, 16, 8, G), F32),
                pltpu.VMEM((groups, 16, 8, G), F32),
                pltpu.VMEM((groups, 8, 8, G), F32),
                pltpu.SemaphoreType.DMA((5,)),
                pltpu.SemaphoreType.DMA((rounds, n - 1)),
                pltpu.SemaphoreType.DMA((rounds, n - 1)),
                pltpu.SemaphoreType.DMA((rounds,)),
                pltpu.SemaphoreType.DMA((rounds,)),
                pltpu.SemaphoreType.DMA((messages,)),
                pltpu.SemaphoreType.DMA((messages,)),
                pltpu.SemaphoreType.DMA((2,)),
            ],
            compiler_params=pltpu.CompilerParams(
                collective_id=0, has_side_effects=True, vmem_limit_bytes=VMEM_BYTES
            ),
        )(boundary, gate_stack, coupling).T

    return jax.shard_map(
        on_device, mesh=mesh, in_specs=(P("cuts", "bits", None), P(), P()), out_specs=P("bits", "cuts"), check_vma=False
    )
```

```python
import functools

import jax
import jax.numpy as jnp
from jax import lax
from jax.experimental import pallas as pl
from jax.experimental.pallas import tpu as pltpu
from jax.sharding import PartitionSpec as P

MESH = pl.DeviceIdType.MESH
CYC_A = 4
CYC_B = 4
CYC_C = 5
G = 128
F32 = jnp.float32
BF16 = jnp.bfloat16
VMEM_BYTES = 63 * 2**20


def split(x):
    hi = x.astype(BF16)
    lo = (x - hi.astype(F32)).astype(BF16)
    return hi, lo


def left_gate(w_ref, index, x):
    hi, lo = w_ref[index, 0], w_ref[index, 1]
    xh, xl = split(x)
    return jnp.dot(
        jnp.concatenate([hi, hi, lo], 1), jnp.concatenate([xh, xl, xh], 0), preferred_element_type=F32
    )


def right_gate(w_ref, index, x):
    row = jnp.concatenate([w_ref[index, 0], w_ref[index, 1]], 1)
    rhs = jnp.concatenate([row, row], 0)
    xh, xl = split(x)
    y = jnp.dot(jnp.concatenate([xh, xl], 1), rhs, preferred_element_type=F32)
    return y[:, :G] + y[:, G:]


def lane_blocks(shape, width):
    return lax.broadcasted_iota(jnp.int32, shape, 1) // width


def transpose_blocks(parts, width):
    n = len(parts)
    parts = list(parts)
    block = lane_blocks(parts[0].shape, width)
    m = 1
    while m < n:
        zero = (block // m) % 2 == 0
        for g in range(n):
            if g & m == 0:
                lo, hi = parts[g], parts[g | m]
                parts[g] = jnp.where(zero, lo, pltpu.roll(hi, m * width, 1))
                parts[g | m] = jnp.where(zero, pltpu.roll(lo, G - m * width, 1), hi)
        m *= 2
    return parts


def repack(src, dst, n, width):
    groups = 16 // n
    for p in range(groups):
        for q in range(groups):
            parts = transpose_blocks([src[p, q * n + h] for h in range(n)], width)
            for g in range(n):
                dst[q, p * n + g] = parts[g]


def kernel(
    n, nb, x_hbm, gate_hbm, cpl_hbm, out_ref,
    x_in, gate_ref, cpl_ref, x, wt, wl, wm, tab, tmp, rs_buf, red, swp, sbuf, rbuf, mp, tp, in0,
    in_sem, rs_send, rs_recv, swp_send, swp_recv, fin_send, fin_recv, in0_sem,
):
    spans = ((0, 4), (4, 3 * CYC_A + 1), (3 * CYC_A + 1, gate_ref.shape[0]))
    loads = [
        pltpu.make_async_copy(gate_hbm.at[pl.ds(a, b - a)], gate_ref.at[pl.ds(a, b - a)], in_sem.at[i])
        for i, (a, b) in enumerate(spans)
    ]
    load_cpl = pltpu.make_async_copy(cpl_hbm, cpl_ref, in_sem.at[3])
    load_x = pltpu.make_async_copy(x_hbm.at[0], x_in, in_sem.at[4])
    loads[0].start()
    load_x.start()
    loads[1].start()
    load_cpl.start()

    me = lax.axis_index("cuts")
    bit = lax.axis_index("bits")
    width = G // n
    groups = 16 // n
    top_mask = nb // 2
    par_top = (bit // top_mask) % 2
    par_low = bit % 2
    mate_top = bit + (1 - 2 * par_top) * top_mask
    mate_low = bit + 1 - 2 * par_low
    out_base = (1 - par_top) * 8
    stay_base = par_top * 8

    barrier = pltpu.get_barrier_semaphore()
    for d in range(1, n):
        pl.semaphore_signal(barrier, inc=1, device_id=(bit, lax.rem(me + d, n)), device_id_type=MESH)
    pl.semaphore_signal(barrier, inc=1, device_id=(mate_top, me), device_id_type=MESH)
    pl.semaphore_signal(barrier, inc=1, device_id=(mate_low, me), device_id_type=MESH)

    rounds = 2 * (8 // n) if n <= 8 else 1

    def share(ref, base, k, r):
        if n <= 8:
            return ref.at[base + k * (rounds // 2) + r // 2, pl.ds(r % 2 * 8, 8)]
        cut = n // 8
        return ref.at[base + k // cut, pl.ds((k % cut) * (16 // cut), 16 // cut)]

    eye = jnp.where(
        lax.broadcasted_iota(jnp.int32, (G, G), 0) == lax.broadcasted_iota(jnp.int32, (G, G), 1), F32(0.9), F32(0.0)
    )

    def put(w_ref, index, value):
        hi, lo = split(value)
        w_ref[index, 0] = hi
        w_ref[index, 1] = lo

    def reorder(load):
        return jnp.concatenate([load(c) for c in range(16)], 0)

    def prep_top(index, gate):
        put(wt, index, (eye + 0.45 * gate_ref[gate]).T)

    def prep_lane(index, gate):
        put(wl, index, eye + 0.45 * gate_ref[gate])

    def prep_mid(index, gate, natural=False):
        rows = reorder(lambda c: gate_ref[gate, pl.ds(c, 8, stride=16), :])
        if natural:
            diag = tmp_eye()
            put(wm, index, diag + 0.45 * rows.T)
        else:
            tmp[...] = rows.T
            put(wm, index, eye + 0.45 * reorder(lambda c: tmp[pl.ds(c, 8, stride=16), :]))

    def tmp_eye():
        r = lax.broadcasted_iota(jnp.int32, (G, G), 0)
        c = lax.broadcasted_iota(jnp.int32, (G, G), 1)
        return jnp.where((c % 8) * 16 + c // 8 == r, F32(0.9), F32(0.0))

    def prep_table(index, packed):
        value = reorder(lambda c: cpl_ref[index, pl.ds(c, 8, stride=16), :])
        if packed:
            value = jnp.where(lane_blocks((G, G), width) == me, value, 0.0)
            m = 1
            while m < n:
                value = value + pltpu.roll(value, m * width, 1)
                m *= 2
        tab[index] = value

    def prep_layer(layer):
        prep_top(layer, 3 * layer)
        prep_lane(layer, 3 * layer + 1)
        prep_mid(layer, 3 * layer + 2)

    def prep_layers(first, count):
        pl.loop(first, first + count)(prep_layer)

    def top(layer, load=lambda t: x[:, t].reshape(G, G)):
        for j in range(0, 16, 2):
            y = left_gate(wt, layer, jnp.concatenate([load(j), load(j + 1)], 1))
            for u in range(2):
                x[:, j + u] = y[:, u * G:(u + 1) * G].reshape(16, 8, G)

    def lane_mid(layer, blocks):
        table = tab[layer]
        for j in range(0, len(blocks), 2):
            y = right_gate(wl, layer, jnp.concatenate([x[blocks[j + u]].reshape(G, G) for u in range(2)], 0))
            y = jnp.concatenate([y[u * G:(u + 1) * G] * table for u in range(2)], 1)
            y = left_gate(wm, layer, y)
            for u in range(2):
                x[blocks[j + u]] = y[:, u * G:(u + 1) * G].reshape(16, 8, G)

    loads[0].wait()
    prep_top(0, 0)
    load_x.wait()
    loads[2].start()
    top(0, lambda t: x_in[pl.ds(t, G, stride=16), :])
    prep_lane(0, 1)
    prep_mid(0, 2)
    prep_top(1, 3)
    load_cpl.wait()
    prep_table(0, False)
    loads[1].wait()

    for layer in range(CYC_A - 1):
        lane_mid(layer, range(16))
        top(layer + 1)
        prep_lane(layer + 1, 3 * layer + 4)
        prep_mid(layer + 1, 3 * layer + 5)
        prep_top(layer + 2, 3 * layer + 6)
        prep_table(layer + 1, False)

    rs = []
    for r in range(rounds):
        if rounds == 4:
            if r % 2 == 0:
                lane_mid(CYC_A - 1, [out_base + 2 * i + r // 2 for i in range(4)])
        elif r == 0:
            lane_mid(CYC_A - 1, [out_base + i for i in range(8)])
        if r == 0:
            pl.semaphore_wait(barrier, n + 1)
        rs.append([])
        for d in range(1, n):
            to = lax.rem(me + d, n)
            rs[r].append(pltpu.make_async_remote_copy(
                src_ref=share(x, out_base, to, r), dst_ref=rs_buf.at[r, d - 1],
                send_sem=rs_send.at[r, d - 1], recv_sem=rs_recv.at[r, d - 1],
                device_id=(bit, to), device_id_type=MESH,
            ))
            rs[r][-1].start()
    lane_mid(CYC_A - 1, [stay_base + i for i in range(8)])
    loads[2].wait()

    swaps = []
    for r in range(rounds):
        for copy in rs[r]:
            copy.wait_recv()
        total = share(x, out_base, me, r)[...]
        for d in range(1, n):
            total = total + rs_buf[r, d - 1]
        red[r] = total
        swaps.append(pltpu.make_async_remote_copy(
            src_ref=red.at[r], dst_ref=swp.at[r], send_sem=swp_send.at[r], recv_sem=swp_recv.at[r],
            device_id=(mate_top, me), device_id_type=MESH,
        ))
        swaps[r].start()

    prep_layers(CYC_A, CYC_B)

    @pl.loop(CYC_A, CYC_A + CYC_B - 1)
    def _(layer):
        prep_table(layer, False)

    @pl.loop(CYC_A + CYC_B - 1, CYC_A + CYC_B + CYC_C)
    def _(layer):
        prep_table(layer, True)

    last = CYC_A + CYC_B
    @pl.loop(0, CYC_C)
    def _(turn):
        prep_top(last + turn, 3 * last + 2 * turn)

    @pl.loop(0, CYC_C - 1)
    def _(turn):
        prep_mid(last + turn, 3 * last + 2 * turn + 1)

    prep_mid(last + CYC_C - 1, 3 * last + 2 * (CYC_C - 1) + 1, natural=True)

    for r in range(rounds):
        for copy in rs[r]:
            copy.wait_send()
    for j in range(8):
        x[out_base + j] = jnp.zeros((16, 8, G), F32)
    for r in range(rounds):
        swaps[r].wait()
        share(x, out_base, me, r)[...] = swp[r]

    top(CYC_A)

    for layer in range(CYC_A, CYC_A + CYC_B - 1):
        lane_mid(layer, range(16))
        top(layer + 1)

    final = CYC_A + CYC_B - 1

    def send(src, dst, index, to):
        copy = pltpu.make_async_remote_copy(
            src_ref=src, dst_ref=dst, send_sem=fin_send.at[index], recv_sem=fin_recv.at[index],
            device_id=(bit, to), device_id_type=MESH,
        )
        copy.start()
        return copy

    near = (me + 1 - 2 * (me % 2), me + 2 - 4 * (me // 2))
    far = 3 - me
    first, second, third = [], [], []
    for p in range(groups):
        y = right_gate(wl, final, x[pl.ds(p * n, n)].reshape(n * G, G))
        parts = transpose_blocks([y[g * G:(g + 1) * G] for g in range(n)], width)
        for k in range(n):
            sbuf[k, p] = parts[k].reshape(16, 8, G)
        if n == 4:
            first.append(send(sbuf.at[far, p], rbuf.at[0, p], p, near[p % 2]))
    if n == 4:
        for p in range(groups):
            second.append(send(sbuf.at[near[p % 2], p], rbuf.at[1, p], groups + p, near[p % 2]))
        for p in range(groups):
            first[p].wait_recv()
            to = near[1 - p % 2]
            sbuf[to, p] = sbuf[to, p] + rbuf[0, p]
            third.append(send(sbuf.at[to, p], rbuf.at[2, p], 2 * groups + p, to))
        terms = (1, 2)
    else:
        for d in range(1, n):
            to = lax.rem(me + d, n)
            second.append(send(sbuf.at[to], rbuf.at[d - 1], d - 1, to))
        terms = range(n - 1)
    for copy in second + third:
        copy.wait_recv()
    fin = first + second + third

    def mid_packed(layer, load):
        table = tab[layer]
        y = jnp.concatenate([load(p) * table for p in range(groups)], 1)
        return left_gate(wm, layer, y)

    def load_sum(p):
        total = sbuf[me, p]
        for d in terms:
            total = total + rbuf[d, p]
        return total.reshape(G, G)

    def put_packed(ref, y):
        for p in range(groups):
            ref[p] = y[:, p * G:(p + 1) * G].reshape(16, 8, G)

    put_packed(mp, mid_packed(final, load_sum))
    repack(mp, tp, n, width)

    swap_low = pltpu.make_async_remote_copy(
        src_ref=tp.at[:, pl.ds((1 - par_low) * 8, 8)], dst_ref=in0,
        send_sem=in0_sem.at[0], recv_sem=in0_sem.at[1],
        device_id=(mate_low, me), device_id_type=MESH,
    )
    swap_low.start()
    for copy in fin:
        copy.wait_send()
    swap_low.wait()
    tp[:, pl.ds((1 - par_low) * 8, 8)] = in0[...]

    def top_packed(layer):
        y = jnp.concatenate([tp[p].reshape(G, G) for p in range(groups)], 1)
        put_packed(tp, left_gate(wt, layer, y))
        repack(tp, mp, n, width)

    for layer in range(last, last + CYC_C - 1):
        top_packed(layer)
        put_packed(mp, mid_packed(layer, lambda p: mp[p].reshape(G, G)))
        repack(mp, tp, n, width)

    end = last + CYC_C - 1
    top_packed(end)
    y = mid_packed(end, lambda p: mp[p].reshape(G, G))
    for p in range(groups):
        part = y[:, p * G:(p + 1) * G]
        part = part.T
        for g in range(n):
            out_ref[:, (p * n + g) * G:(p * n + g + 1) * G] = part[g * width:(g + 1) * width]


def solution(mesh):
    n, nb = mesh.shape["cuts"], mesh.shape["bits"]
    groups = 16 // n
    rounds = 2 * (8 // n) if n <= 8 else 1
    part = (rounds, 8 if n <= 8 else 16 // (n // 8), 8, G)
    messages = 3 * groups if n == 4 else n - 1

    def on_device(boundary, gate_stack, coupling):
        gates, tables = gate_stack.shape[0], coupling.shape[0]
        layers = CYC_A + CYC_B + CYC_C
        return pl.pallas_call(
            functools.partial(kernel, n, nb),
            out_shape=jax.ShapeDtypeStruct((G // n, boundary.shape[1]), F32),
            in_specs=[pl.BlockSpec(memory_space=pltpu.HBM)] * 3,
            out_specs=pl.BlockSpec(memory_space=pltpu.VMEM),
            scratch_shapes=[
                pltpu.VMEM(boundary.shape[1:], F32),
                pltpu.VMEM((gates, G, G), F32),
                pltpu.VMEM((tables, G, G), F32),
                pltpu.VMEM((16, 16, 8, G), F32),
                pltpu.VMEM((layers, 2, G, G), BF16),
                pltpu.VMEM((CYC_A + CYC_B, 2, G, G), BF16),
                pltpu.VMEM((layers, 2, G, G), BF16),
                pltpu.VMEM((layers, G, G), F32),
                pltpu.VMEM((G, G), F32),
                pltpu.VMEM((rounds, n - 1) + part[1:], F32),
                pltpu.VMEM(part, F32),
                pltpu.VMEM(part, F32),
                pltpu.VMEM((n, groups, 16, 8, G), F32),
                pltpu.VMEM((n - 1, groups, 16, 8, G), F32),
                pltpu.VMEM((groups, 16, 8, G), F32),
                pltpu.VMEM((groups, 16, 8, G), F32),
                pltpu.VMEM((groups, 8, 8, G), F32),
                pltpu.SemaphoreType.DMA((5,)),
                pltpu.SemaphoreType.DMA((rounds, n - 1)),
                pltpu.SemaphoreType.DMA((rounds, n - 1)),
                pltpu.SemaphoreType.DMA((rounds,)),
                pltpu.SemaphoreType.DMA((rounds,)),
                pltpu.SemaphoreType.DMA((messages,)),
                pltpu.SemaphoreType.DMA((messages,)),
                pltpu.SemaphoreType.DMA((2,)),
            ],
            compiler_params=pltpu.CompilerParams(
                collective_id=0, has_side_effects=True, vmem_limit_bytes=VMEM_BYTES
            ),
        )(boundary, gate_stack, coupling).T

    return jax.shard_map(
        on_device, mesh=mesh, in_specs=(P("cuts", "bits", None), P(), P()), out_specs=P("bits", "cuts"), check_vma=False
    )
```
